256 devices in a mesh: rel: 16 (over x, y), node: 16 (over z, core).
Axes of the slice: x: 4, y: 4, z: 8, core: 2. Of those that a mesh axis runs over, the one named last changes fastest.
Arguments:
- out_adjoint: bfloat16 [16, 1024, 512], P('node', 'rel'), may hold values from -6 to 6
- layer_input: bfloat16 [16, 1024, 512], P('node'), may hold values from -0.15625 to 0.15625
- rel_weights: bfloat16 [32, 512, 512], P('rel'), may hold values from -0.25 to 0.25
- self_weight: bfloat16 [512, 512], replicated, may hold values from -0.25 to 0.25
- tile_values: bfloat16 [16, 1024, 128, 128], P('rel', 'node'), may hold values from 0 to 0.039794922
- tile_rel: int32 [16, 1024], P('rel', 'node'), may hold values from 0 to 1
- tile_target: int32 [16, 1024], P('rel', 'node'), may hold values from 0 to 7
- tile_src: int32 [16, 1024], P('rel', 'node'), may hold values from 0 to 7
- tile_dest: int32 [16, 1024, 1], P('rel', 'node'), may hold values from 0 to 15; in each aligned block of 64 rows (0 to 63, 64 to 127, ..., all dimensions but the last counted through in order) at most 8 rows name the same one
Outputs:
- rel_weight_grad: float32 [32, 512, 512], P('rel', 'node')
- d_source: bfloat16 [16, 1024, 512], P('node', 'rel')
The draws below stay inside these ranges and needn't reach their ends.
Inputs may be any that keep to these rules, and one draw needn't show every extreme that they name: `tile_dest`: among the 64 tiles of one device, at most 8 name the same node shard, and some node shard is named by exactly 8 of them.
All inputs are finite; a program needn't handle non-finite values.
Results may differ from the reference program's by a relative error of at most 0.0056.
Values may be sent and summed in bfloat16 or wider, within the bound.
A program may use at most 128 MiB of HBM per device.

```python
import math
import jax
import jax.numpy as jnp
import numpy as np
from jax import lax

D = 512
TB = 128
ROWS_DEV = 1024
REL_DEV = 2
BLOCKS = 8
CAP = 8
TILES_DEV = 64
RELS = 32
NODES = 16384
N_REL = 16
N_NODE = 16


def plant(drawn, own_key, smallest, largest):
    longest = drawn.shape.index(max(drawn.shape))
    spots = []
    for shift in (0, 1):
        where = [jax.random.randint(jax.random.fold_in(own_key, axis), (), 0, length) for axis, length in enumerate(drawn.shape)]
        where[longest] = (where[longest] + shift) % drawn.shape[longest]
        spots.append(tuple(where))
    return drawn.at[spots[0]].set(smallest).at[spots[1]].set(largest)


def strengthened(drawn, own_key, source, target, parts, factor):
    owner, partner = [(jnp.arange(drawn.shape[position]) // (drawn.shape[position] // parts)).reshape([-1 if axis == position else 1 for axis in range(drawn.ndim)]) for position in (source, target)]
    chosen = jax.random.permutation(own_key, parts)[partner]
    strong = (owner == chosen) | (owner == (partner + parts // 2) % parts)
    return jnp.where(strong, factor * drawn, drawn)


def shard_levels(rng, shape, split, smallest, high):
    def one(position, parts):
        heights = jax.random.uniform(jax.random.fold_in(jax.random.fold_in(rng, 6), position), (parts,), jnp.float32, smallest / len(split), high / len(split))
        return jnp.repeat(jnp.exp(heights), shape[position] // parts).reshape((-1,) + (1,) * (len(shape) - position - 1))

    loudness = one(*split[0])
    for cut in split[1:]:
        loudness = loudness * one(*cut)
    return loudness


def deal_out(own_key, own, number, rows, amount, top, bound, skew):
    ranking = jax.random.permutation(own_key, amount)
    crowded, usual = shares(amount, rows * top, bound, skew, True), shares(amount, rows * top, bound, skew, False)
    places = jnp.arange(amount)

    def named(sizes, turn):
        used = int((sizes > 0).sum())
        fixed = max(1, used // 4)
        moved = fixed + (places - fixed + turn * (used - fixed)) % max(1, amount - fixed)
        return jnp.zeros((amount,), jnp.int32).at[ranking[jnp.where(places < fixed, places, moved)]].set(jnp.asarray(sizes, jnp.int32))

    sizes = jnp.where(number % 4 == 0, named(crowded, number // 4), named(usual, number - number // 4 - 1))
    mixed = jax.random.permutation(jax.random.fold_in(own, 3), amount)
    source_of, receiver = mixed[0:amount // 2 * 2:2], mixed[1:amount // 2 * 2:2]
    room = jnp.minimum(sizes[source_of] - 1, bound - sizes[receiver]) // 2
    room = jnp.where((source_of == ranking[0]) | (receiver == ranking[0]) | (sizes[receiver] == 0), 0, jnp.maximum(room, 0))
    moved = jax.random.randint(jax.random.fold_in(own, 4), (amount // 2,), 0, 1 << 20) % (room + 1)
    sizes = sizes.at[source_of].add(-moved).at[receiver].add(moved)
    items = jnp.searchsorted(jnp.cumsum(sizes), jnp.arange(rows * top), side="right").astype(jnp.int32)
    grid = items.reshape(top, rows).T
    grid = grid[jax.random.permutation(jax.random.fold_in(own, 1), rows)]
    turn = jax.random.randint(jax.random.fold_in(own, 2), (rows, 1), 0, top)
    return jnp.take_along_axis(grid, (jnp.arange(top)[None, :] + turn) % top, axis=1)


def shares(number_of, total, reach, lean, full):
    loads = [(1 << 20) // math.isqrt(grade ** lean) + 1 for grade in range(1, number_of + 1)]
    largest = reach if full else min(reach, max(-(-total // number_of), total * loads[0] // sum(loads)))
    least = 1 if total - largest >= number_of - 1 else 0
    holding, rest = [largest] + [least] * (number_of - 1), total - largest - least * (number_of - 1)
    while rest > 0:
        free = [i for i in range(1, number_of) if holding[i] < largest] or [i for i in range(1, number_of) if holding[i] < reach]
        whole, left = sum([loads[i] for i in free]), rest
        for i in free:
            addition = min(reach - holding[i], max(1, left * loads[i] // whole), rest)
            holding[i] = holding[i] + addition
            rest = rest - addition
    return np.array(holding)


def centred(rng, dims, spread, reach, split=(), dtype=jnp.bfloat16):
    gain = shard_levels(rng, dims, split, -0.22, 0.18) if split else 1.0
    values = jax.random.normal(rng, dims, jnp.float32) * spread * gain
    return jnp.minimum(jnp.maximum(values, -reach), reach).astype(dtype)


def bell_draw_with(own_key, dims, deviation, reach, pieces, heavy, held_as=jnp.bfloat16):
    entries = deviation * jax.random.normal(own_key, dims, jnp.float32)
    if pieces:
        entries = entries * shard_levels(own_key, dims, pieces, -0.22, 0.18)
    return jnp.clip(strengthened(entries, jax.random.fold_in(own_key, 3), *heavy), -reach, reach).astype(held_as)


def setup_inputs(seed: int = 0) -> dict:
    splits = jax.random.split(jax.random.key(seed), 10)
    out_adjoint = centred(splits[0], (N_NODE, ROWS_DEV, D), 1.0, 6.0, ((0, 16), (1, 16)))
    layer_input = bell_draw_with(splits[1], (N_NODE, ROWS_DEV, D), 0.02, 0.15625, ((0, 16),), (0, 2, 16, 2.0))
    rel_weights = centred(splits[2], (RELS, D, D), D ** -0.5, 0.25, ((0, 16),))
    self_weight = centred(splits[3], (D, D), D ** -0.5, 0.25)
    tile_values = jnp.clip(0.039794922 * jax.random.uniform(splits[4], (N_REL, N_NODE * TILES_DEV, TB, TB), jnp.float32) ** shard_levels(splits[4], (N_REL, N_NODE * TILES_DEV, TB, TB), ((0, 16), (1, 16)), -0.2, 0.2), 0.0, 0.039794922).astype(jnp.bfloat16)
    tile_rel = plant(jax.random.randint(splits[5], (N_REL, N_NODE * TILES_DEV), 0, REL_DEV), jax.random.fold_in(splits[5], 1), 0, REL_DEV - 1).astype(jnp.int32)
    tile_target = plant(jax.random.randint(splits[6], (N_REL, N_NODE * TILES_DEV), 0, BLOCKS), jax.random.fold_in(splits[6], 1), 0, BLOCKS - 1).astype(jnp.int32)
    tile_src = plant(jax.random.randint(splits[7], (N_REL, N_NODE * TILES_DEV), 0, BLOCKS), jax.random.fold_in(splits[7], 1), 0, BLOCKS - 1).astype(jnp.int32)
    tile_dest_keys = jax.random.split(jax.random.fold_in(splits[8], 1), N_REL * (N_NODE * TILES_DEV) // TILES_DEV)
    tile_dest_turns = jax.random.permutation(jax.random.fold_in(splits[8], 3), N_REL * (N_NODE * TILES_DEV) // TILES_DEV)
    tile_dest = jax.vmap(lambda own, number: deal_out(jax.random.fold_in(splits[8], 2), own, number, TILES_DEV, N_NODE, 1, CAP, 2))(tile_dest_keys, tile_dest_turns).reshape((N_REL, N_NODE * TILES_DEV, 1))
    return dict(out_adjoint=out_adjoint, layer_input=layer_input, rel_weights=rel_weights, self_weight=self_weight, tile_values=tile_values, tile_rel=tile_rel, tile_target=tile_target, tile_src=tile_src, tile_dest=tile_dest)


def reference(out_adjoint, layer_input, rel_weights, self_weight, tile_values, tile_rel, tile_target, tile_src, tile_dest):
    adjoint_blocks = out_adjoint.reshape(N_NODE * BLOCKS, TB, D)
    inputs = layer_input.reshape(NODES, D).astype(jnp.float32)
    owners = tile_dest[..., 0]
    sender = (jnp.arange(N_NODE * TILES_DEV) // TILES_DEV).astype(jnp.int32)
    weights_grouped = rel_weights.reshape(N_REL, REL_DEV, D, D)

    def one_group(carry, per_group):
        values, relation, target, source, owner, weights = per_group
        chosen = adjoint_blocks[(sender * BLOCKS + target).astype(jnp.int32)].astype(jnp.float32)
        partial_value = jnp.einsum("tij,tid->tjd", values.astype(jnp.float32), chosen).astype(jnp.bfloat16)
        partial_value = lax.optimization_barrier(partial_value)
        bucket = (relation * (N_NODE * BLOCKS) + owner * BLOCKS + source).astype(jnp.int32)
        summed = jax.ops.segment_sum(partial_value.astype(jnp.float32), bucket, num_segments=REL_DEV * N_NODE * BLOCKS)
        rounded = summed.reshape(REL_DEV, NODES, D).astype(jnp.bfloat16)
        rounded = lax.optimization_barrier(rounded)
        aggregated = rounded.astype(jnp.float32)
        grads = jnp.einsum("vi,rvj->rij", inputs, aggregated)
        carry = carry + jnp.einsum("rvj,rij->vi", aggregated, weights.astype(jnp.float32))
        return carry, grads

    start = jnp.dot(out_adjoint.reshape(NODES, D), self_weight.T, preferred_element_type=jnp.float32)
    total, grads = lax.scan(one_group, start, (tile_values, tile_rel, tile_target, tile_src, owners, weights_grouped))
    return grads.reshape(RELS, D, D), total.astype(jnp.bfloat16).reshape(N_NODE, ROWS_DEV, D)
```

```python
import jax
import jax.numpy as jnp
from jax import lax
from jax.experimental import pallas as pl
from jax.experimental.pallas import tpu as pltpu
from jax.sharding import PartitionSpec as P

MESH = pl.DeviceIdType.MESH
ANY = pl.BlockSpec(memory_space=pl.ANY)
VMEM = pl.BlockSpec(memory_space=pltpu.VMEM)
SMEM = pl.BlockSpec(memory_space=pltpu.SMEM)

SIDE = 4
NODES = 16
ROWS = 64
QUARTER = 128
TILES = 64
EDGE = 128
FEATURE = 512
BLOCKS = 8
CHUNK = 16


def place():
    rel, node = lax.axis_index("rel"), lax.axis_index("node")
    return (
        lax.div(rel, SIDE),
        lax.rem(rel, SIDE),
        lax.div(node, 2),
        lax.rem(node, 2),
        rel,
        node,
    )


def quarter_of(node):
    return lax.rem(lax.div(node, 2), 2) * 2 + lax.rem(node, 2)


def greet(x, y, rel, node):
    barrier = pltpu.get_barrier_semaphore()

    def call(there_rel, there_node):
        pl.semaphore_signal(
            barrier, inc=1, device_id=(there_rel, there_node), device_id_type=MESH
        )

    for k in range(1, SIDE):
        call(lax.rem(x + k, SIDE) * SIDE + y, node)
        call(x * SIDE + lax.rem(y + k, SIDE), node)
    for k in range(1, NODES):
        call(rel, lax.rem(node + k, NODES))
    pl.semaphore_wait(barrier, 2 * (SIDE - 1) + NODES - 1)


def push(src, dst, send, recv, there):
    copy = pltpu.make_async_remote_copy(
        src_ref=src,
        dst_ref=dst,
        send_sem=send,
        recv_sem=recv,
        device_id=there,
        device_id_type=MESH,
    )
    copy.start()
    return copy


def gather_kernel(
    adj,
    layer,
    tiles,
    meta,
    t_all,
    a_all,
    x_all,
    m_all,
    local_sem,
    a_send,
    a_recv,
    x_send,
    x_recv,
    z_send,
    z_recv,
    t_send,
    t_recv,
    s_send,
    s_recv,
    m_send,
    m_recv,
):
    x, y, z, c, rel, node = place()
    half = ROWS // 2
    own = 1 + c
    sibling = (rel, z * 2 + (1 - c))
    beside = lax.rem(z + 7 + 2 * c, 8)
    away = 3 * (1 - c)
    quarter = quarter_of(node)

    def x_peer(k):
        return (lax.rem(x + k, SIDE) * SIDE + y, node)

    def y_peer(k):
        return (x * SIDE + lax.rem(y + k, SIDE), node)

    greet(x, y, rel, node)

    a_first = []
    for k in range(1, SIDE):
        a_first.append(
            push(
                adj.at[pl.ds(0, half)],
                a_all.at[own, x, y, pl.ds(0, half)],
                a_send.at[0, k - 1],
                a_recv.at[0, k - 1],
                x_peer(k),
            )
        )
        a_first.append(
            push(
                adj.at[pl.ds(half, half)],
                a_all.at[own, x, y, pl.ds(half, half)],
                a_send.at[1, k - 1],
                a_recv.at[1, k - 1],
                y_peer(k),
            )
        )
    a_own = pltpu.make_async_copy(adj, a_all.at[own, x, y], local_sem.at[0])
    a_own.start()

    z_copies = []
    for k in range(1, NODES):
        there = lax.rem(node + k, NODES)
        column = pl.multiple_of(quarter_of(there) * QUARTER, QUARTER)
        z_copies.append(
            push(
                layer.at[pl.ds(rel * ROWS, ROWS), pl.ds(column, QUARTER)],
                x_all.at[node, x, y],
                z_send.at[k - 1],
                z_recv.at[k - 1],
                (rel, there),
            )
        )
    x_own = pltpu.make_async_copy(
        layer.at[
            pl.ds(rel * ROWS, ROWS),
            pl.ds(pl.multiple_of(quarter * QUARTER, QUARTER), QUARTER),
        ],
        x_all.at[node, x, y],
        local_sem.at[1],
    )
    x_own.start()

    m_copies = [push(meta, m_all.at[own], m_send.at[0], m_recv.at[0], sibling)]
    m_own = pltpu.make_async_copy(meta, m_all.at[own], local_sem.at[2])
    m_own.start()
    t_own = pltpu.make_async_copy(tiles, t_all.at[own], local_sem.at[3])
    t_own.start()
    t_far = []
    for h in range(2):
        there = (rel, beside * 2 + h)
        m_copies.append(
            push(meta, m_all.at[away], m_send.at[1 + h], m_recv.at[1 + c], there)
        )
        part = pl.ds(h * (TILES // 2), TILES // 2)
        t_far.append(
            push(
                tiles.at[part],
                t_all.at[away, part],
                t_send.at[h],
                t_recv.at[c],
                there,
            )
        )
    t_near = push(tiles, t_all.at[own], s_send.at[0], s_recv.at[0], sibling)

    def arrival(ref, sem):
        pltpu.make_async_copy(ref, ref, sem).wait()

    a_own.wait()
    for copy in a_first:
        copy.wait()
    a_second = []
    for k in range(1, SIDE):
        mine = a_all.at[own, :, y, pl.ds(0, half)]
        a_second.append(
            push(mine, mine, a_send.at[2, k - 1], a_recv.at[2, k - 1], y_peer(k))
        )
        mine = a_all.at[own, x, :, pl.ds(half, half)]
        a_second.append(
            push(mine, mine, a_send.at[3, k - 1], a_recv.at[3, k - 1], x_peer(k))
        )

    x_own.wait()
    for copy in z_copies:
        copy.wait()
    x_first = []
    for k in range(1, SIDE):
        mine = x_all.at[pl.ds(0, 8), x, y]
        x_first.append(
            push(mine, mine, x_send.at[0, k - 1], x_recv.at[0, k - 1], x_peer(k))
        )
        mine = x_all.at[pl.ds(8, 8), x, y]
        x_first.append(
            push(mine, mine, x_send.at[1, k - 1], x_recv.at[1, k - 1], y_peer(k))
        )

    for copy in a_second:
        copy.wait()
    a_far = []
    for h in range(2):
        part = pl.ds(2 * h, 2)
        a_far.append(
            push(
                a_all.at[own, part],
                a_all.at[away, part],
                t_send.at[2 + h],
                t_recv.at[2 + c],
                (rel, beside * 2 + h),
            )
        )
    a_near = push(
        a_all.at[own], a_all.at[own], s_send.at[1], s_recv.at[1], sibling
    )

    for copy in x_first:
        copy.wait()
    x_second = []
    for k in range(1, SIDE):
        mine = x_all.at[pl.ds(0, 8), :, y]
        x_second.append(
            push(mine, mine, x_send.at[2, k - 1], x_recv.at[2, k - 1], y_peer(k))
        )
        mine = x_all.at[pl.ds(8, 8), x]
        x_second.append(
            push(mine, mine, x_send.at[3, k - 1], x_recv.at[3, k - 1], x_peer(k))
        )

    onward = []
    mine = pl.ds(c * (TILES // 2), TILES // 2)
    rows = pl.ds(2 * c, 2)
    for sender, slot in ((0, 3), (1, 0)):
        arrival(t_all.at[slot, mine], t_recv.at[sender])
        onward.append(
            push(
                t_all.at[slot, mine],
                t_all.at[slot, mine],
                s_send.at[2 + sender],
                s_recv.at[2 + sender],
                sibling,
            )
        )
    for sender, slot in ((0, 3), (1, 0)):
        arrival(a_all.at[slot, rows], t_recv.at[2 + sender])
        onward.append(
            push(
                a_all.at[slot, rows],
                a_all.at[slot, rows],
                s_send.at[4 + sender],
                s_recv.at[4 + sender],
                sibling,
            )
        )

    for copy in t_far + a_far:
        copy.wait_send()
    other = 2 - c
    t_near.wait_send()
    a_near.wait_send()
    arrival(t_all.at[other], s_recv.at[0])
    arrival(a_all.at[other], s_recv.at[1])
    theirs = pl.ds((1 - c) * (TILES // 2), TILES // 2)
    their_rows = pl.ds(2 * (1 - c), 2)
    for copy in onward:
        copy.wait_send()
    for sender, slot in ((0, 3), (1, 0)):
        arrival(t_all.at[slot, theirs], s_recv.at[2 + sender])
        arrival(a_all.at[slot, their_rows], s_recv.at[4 + sender])
    for copy in m_copies:
        copy.wait_send()
    arrival(m_all.at[other], m_recv.at[0])
    arrival(m_all.at[3], m_recv.at[1])
    arrival(m_all.at[0], m_recv.at[2])
    m_own.wait()
    t_own.wait()
    for copy in x_second:
        copy.wait()


def gather(adj, layer, tiles, meta):
    dma = pltpu.SemaphoreType.DMA
    return pl.pallas_call(
        gather_kernel,
        out_shape=(
            jax.ShapeDtypeStruct((4, TILES, EDGE, EDGE), jnp.bfloat16),
            jax.ShapeDtypeStruct((4, SIDE, SIDE, ROWS, FEATURE), jnp.bfloat16),
            jax.ShapeDtypeStruct((NODES, SIDE, SIDE, ROWS, QUARTER), jnp.bfloat16),
            jax.ShapeDtypeStruct((4, 8, 128), jnp.int32),
        ),
        in_specs=[ANY] * 4,
        out_specs=(ANY,) * 4,
        scratch_shapes=[
            dma((4,)),
            dma((4, 3)),
            dma((4, 3)),
            dma((4, 3)),
            dma((4, 3)),
            dma((15,)),
            dma((15,)),
            dma((4,)),
            dma((4,)),
            dma((6,)),
            dma((6,)),
            dma((3,)),
            dma((3,)),
        ],
        compiler_params=pltpu.CompilerParams(collective_id=0, has_side_effects=True),
        cost_estimate=pl.CostEstimate(
            flops=0, bytes_accessed=32 << 20, transcendentals=0
        ),
        name="gather_rows_and_tiles",
    )(adj, layer, tiles, meta)


def local_kernel(meta, tiles, a_rows, x_rows, weights, d_out, g_out, aw, d_sum, h_sum):
    step = pl.program_id(0)
    last = pl.num_programs(0) - 1
    quarter = quarter_of(lax.axis_index("node"))
    blocks = 4 * BLOCKS

    @pl.when(step == 0)
    def _():
        d_sum[...] = jnp.zeros_like(d_sum)
        h_sum[...] = jnp.zeros_like(h_sum)
        column = pl.multiple_of(quarter * QUARTER, QUARTER)

        def one(b, carry):
            rows = a_rows[b]
            for r in range(2):
                aw[r, b] = lax.dot_general(
                    weights[r, pl.ds(column, QUARTER), :],
                    rows,
                    (((1,), (1,)), ((), ())),
                    preferred_element_type=jnp.float32,
                ).astype(jnp.bfloat16)
            return carry

        lax.fori_loop(0, blocks, one, 0)

    slot = lax.div(step * CHUNK, TILES)
    first = lax.rem(step * CHUNK, TILES)
    for k in range(CHUNK):
        code = meta[slot, 0, first + k]
        target = slot * BLOCKS + lax.rem(code, BLOCKS)
        relation = lax.rem(lax.div(code, BLOCKS), 2)
        bucket = lax.div(code, 2 * BLOCKS)
        tile = tiles[k]
        d_sum[bucket] += jnp.dot(
            aw[relation, target], tile, preferred_element_type=jnp.float32
        )
        h_sum[relation, target] += jnp.dot(
            tile, x_rows[bucket], preferred_element_type=jnp.float32
        )

    @pl.when(step == last)
    def _():
        def turn(b, carry):
            d_out[b] = d_sum[b].T.astype(jnp.bfloat16)
            return carry

        lax.fori_loop(0, NODES * BLOCKS, turn, 0)
        for r in range(2):

            def add(b, total):
                turned = h_sum[r, b].T.astype(jnp.bfloat16)
                return total + jnp.dot(
                    turned, a_rows[b], preferred_element_type=jnp.float32
                )

            g_out[r] = lax.fori_loop(
                0, blocks, add, jnp.zeros((QUARTER, FEATURE), jnp.float32)
            )


def local(meta, tiles, a_rows, x_rows, weights):
    buckets = NODES * BLOCKS
    steps = 4 * TILES // CHUNK
    return pl.pallas_call(
        local_kernel,
        grid=(steps,),
        out_shape=(
            jax.ShapeDtypeStruct((buckets, EDGE, QUARTER), jnp.bfloat16),
            jax.ShapeDtypeStruct((2, QUARTER, FEATURE), jnp.float32),
        ),
        in_specs=[
            SMEM,
            pl.BlockSpec((CHUNK, EDGE, EDGE), lambda s: (s, 0, 0)),
            VMEM,
            VMEM,
            VMEM,
        ],
        out_specs=(VMEM, VMEM),
        scratch_shapes=[
            pltpu.VMEM((2, 4 * BLOCKS, QUARTER, EDGE), jnp.bfloat16),
            pltpu.VMEM((buckets, QUARTER, EDGE), jnp.float32),
            pltpu.VMEM((2, 4 * BLOCKS, EDGE, QUARTER), jnp.float32),
        ],
        compiler_params=pltpu.CompilerParams(
            vmem_limit_bytes=56 << 20, dimension_semantics=("arbitrary",)
        ),
        name="tile_products",
    )(meta, tiles, a_rows, x_rows, weights)


def reduce_kernel(
    d_part,
    g_part,
    adj,
    self_weight,
    g_out,
    d_out,
    own_a,
    own_b,
    got_a,
    got_b,
    sum_a,
    sum_b,
    next_a,
    next_b,
    total,
    got_z,
    got_g,
    own_term,
    local_sem,
    a_send,
    a_recv,
    z_send,
    z_recv,
    g_send,
    g_recv,
):
    x, y, z, c, rel, node = place()
    quarter = quarter_of(node)
    half = NODES // 2

    def x_peer(k):
        return (lax.rem(x + k, SIDE) * SIDE + y, node)

    def y_peer(k):
        return (x * SIDE + lax.rem(y + k, SIDE), node)

    greet(x, y, rel, node)

    first = []
    for k in range(1, SIDE):
        first.append(
            push(
                d_part.at[pl.ds(0, half), lax.rem(x + k, SIDE)],
                got_a.at[k - 1],
                a_send.at[0, k - 1],
                a_recv.at[0, k - 1],
                x_peer(k),
            )
        )
        first.append(
            push(
                d_part.at[pl.ds(half, half), :, lax.rem(y + k, SIDE)],
                got_b.at[k - 1],
                a_send.at[1, k - 1],
                a_recv.at[1, k - 1],
                y_peer(k),
            )
        )
    mine_a = pltpu.make_async_copy(
        d_part.at[pl.ds(0, half), x], own_a, local_sem.at[0]
    )
    mine_a.start()
    mine_b = pltpu.make_async_copy(
        d_part.at[pl.ds(half, half), :, y], own_b, local_sem.at[1]
    )
    mine_b.start()

    sender = lax.div(z, 2)
    for m in range(4):
        owner = quarter * 4 + m
        rows = g_part.at[:, pl.ds(32 * m, 32), :]

        @pl.when(owner != node)
        def _():
            push(
                rows,
                got_g.at[sender],
                g_send.at[m],
                g_recv.at[sender],
                (rel, owner),
            )

        @pl.when(owner == node)
        def _():
            pltpu.make_async_copy(rows, got_g.at[sender], g_recv.at[sender]).start()

    own_term[...] = lax.dot_general(
        adj[...],
        self_weight[...],
        (((1,), (1,)), ((), ())),
        preferred_element_type=jnp.float32,
    )

    mine_a.wait()
    mine_b.wait()
    for copy in first:
        copy.wait()

    def f32(value):
        return value.astype(jnp.float32)

    def add_first(n, carry):
        for own, got, into in ((own_a, got_a, sum_a), (own_b, got_b, sum_b)):
            value = f32(own[n])
            for k in range(SIDE - 1):
                value = value + f32(got[k, n])
            into[n] = value.astype(jnp.bfloat16)
        return carry

    lax.fori_loop(0, half, add_first, 0)

    second = []
    for k in range(1, SIDE):
        second.append(
            push(
                sum_a.at[:, lax.rem(y + k, SIDE)],
                next_a.at[k - 1],
                a_send.at[2, k - 1],
                a_recv.at[2, k - 1],
                y_peer(k),
            )
        )
        second.append(
            push(
                sum_b.at[:, lax.rem(x + k, SIDE)],
                next_b.at[k - 1],
                a_send.at[3, k - 1],
                a_recv.at[3, k - 1],
                x_peer(k),
            )
        )

    for m in range(4):
        pltpu.make_async_copy(got_g.at[m], got_g.at[m], g_recv.at[m]).wait()
        owner = quarter * 4 + m
        rows = g_part.at[:, pl.ds(32 * m, 32), :]

        @pl.when(owner != node)
        def _():
            pltpu.make_async_remote_copy(
                src_ref=rows,
                dst_ref=got_g.at[sender],
                send_sem=g_send.at[m],
                recv_sem=g_recv.at[sender],
                device_id=(rel, owner),
                device_id_type=MESH,
            ).wait_send()

    g_out[...] = (got_g[0] + got_g[1]) + (got_g[2] + got_g[3])

    for copy in second:
        copy.wait()

    def add_second(n, carry):
        for own, at, got, base in (
            (sum_a, y, next_a, 0),
            (sum_b, x, next_b, half),
        ):
            value = f32(own[n, at])
            for k in range(SIDE - 1):
                value = value + f32(got[k, n])
            total[base + n] = value.astype(jnp.bfloat16)
        return carry

    lax.fori_loop(0, half, add_second, 0)

    z_copies = []
    for k in range(1, NODES):
        there = lax.rem(node + k, NODES)
        z_copies.append(
            push(
                total.at[there],
                got_z.at[node],
                z_send.at[k - 1],
                z_recv.at[k - 1],
                (rel, there),
            )
        )
    mine_z = pltpu.make_async_copy(total.at[node], got_z.at[node], local_sem.at[2])
    mine_z.start()
    mine_z.wait()
    for copy in z_copies:
        copy.wait()
    for q in range(4):
        columns = pl.ds(q * QUARTER, QUARTER)
        value = own_term[:, columns]
        for step in range(4):
            value = value + f32(got_z[(2 * step + q // 2) * 2 + q % 2])
        d_out[:, columns] = value.astype(jnp.bfloat16)


def reduce(d_part, g_part, adj, self_weight):
    dma = pltpu.SemaphoreType.DMA
    half = NODES // 2
    bf16 = jnp.bfloat16
    return pl.pallas_call(
        reduce_kernel,
        out_shape=(
            jax.ShapeDtypeStruct((2, 32, FEATURE), jnp.float32),
            jax.ShapeDtypeStruct((ROWS, FEATURE), bf16),
        ),
        in_specs=[ANY, ANY, VMEM, VMEM],
        out_specs=(VMEM, VMEM),
        scratch_shapes=[
            pltpu.VMEM((half, SIDE, ROWS, QUARTER), bf16),
            pltpu.VMEM((half, SIDE, ROWS, QUARTER), bf16),
            pltpu.VMEM((3, half, SIDE, ROWS, QUARTER), bf16),
            pltpu.VMEM((3, half, SIDE, ROWS, QUARTER), bf16),
            pltpu.VMEM((half, SIDE, ROWS, QUARTER), bf16),
            pltpu.VMEM((half, SIDE, ROWS, QUARTER), bf16),
            pltpu.VMEM((3, half, ROWS, QUARTER), bf16),
            pltpu.VMEM((3, half, ROWS, QUARTER), bf16),
            pltpu.VMEM((NODES, ROWS, QUARTER), bf16),
            pltpu.VMEM((NODES, ROWS, QUARTER), bf16),
            pltpu.VMEM((4, 2, 32, FEATURE), jnp.float32),
            pltpu.VMEM((ROWS, FEATURE), jnp.float32),
            dma((3,)),
            dma((4, 3)),
            dma((4, 3)),
            dma((15,)),
            dma((15,)),
            dma((4,)),
            dma((4,)),
        ],
        compiler_params=pltpu.CompilerParams(
            collective_id=1, has_side_effects=True, vmem_limit_bytes=32 << 20
        ),
        name="sum_terms",
    )(d_part, g_part, adj, self_weight)


def on_device(
    out_adjoint,
    layer_input,
    rel_weights,
    self_weight,
    tile_values,
    tile_rel,
    tile_target,
    tile_src,
    tile_dest,
):
    code = (
        (tile_dest[:, :, 0] * BLOCKS + tile_src) * 2 + tile_rel
    ) * BLOCKS + tile_target
    meta = jnp.pad(code, ((0, 7), (0, 128 - TILES)))
    adj = out_adjoint[0]
    tiles, a_rows, x_rows, codes = gather(adj, layer_input[0], tile_values[0], meta)
    d_part, g_part = local(
        codes,
        tiles.reshape(4 * TILES, EDGE, EDGE),
        a_rows.reshape(4 * BLOCKS, EDGE, FEATURE),
        x_rows.reshape(NODES * BLOCKS, EDGE, QUARTER),
        rel_weights,
    )
    rel_weight_grad, d_source = reduce(
        d_part.reshape(NODES, SIDE, SIDE, ROWS, QUARTER), g_part, adj, self_weight
    )
    return rel_weight_grad, d_source[None]


def solution(mesh):
    return jax.shard_map(
        on_device,
        mesh=mesh,
        in_specs=(
            P("node", "rel", None),
            P("node", None, None),
            P("rel", None, None),
            P(),
            P("rel", "node", None, None),
            P("rel", "node"),
            P("rel", "node"),
            P("rel", "node"),
            P("rel", "node", None),
        ),
        out_specs=(P("rel", "node", None), P("node", "rel", None)),
        check_vma=False,
    )
```

```python
import jax
import jax.numpy as jnp
from jax import lax
from jax.experimental import pallas as pl
from jax.experimental.pallas import tpu as pltpu
from jax.sharding import PartitionSpec as P

MESH = pl.DeviceIdType.MESH
ANY = pl.BlockSpec(memory_space=pl.ANY)
VMEM = pl.BlockSpec(memory_space=pltpu.VMEM)
SMEM = pl.BlockSpec(memory_space=pltpu.SMEM)

SIDE = 4
NODES = 16
ROWS = 64
QUARTER = 128
TILES = 64
EDGE = 128
FEATURE = 512
BLOCKS = 8
CHUNK = 32


def place():
    rel, node = lax.axis_index("rel"), lax.axis_index("node")
    return (
        lax.div(rel, SIDE),
        lax.rem(rel, SIDE),
        lax.div(node, 2),
        lax.rem(node, 2),
        rel,
        node,
    )


def quarter_of(node):
    return lax.rem(lax.div(node, 2), 2) * 2 + lax.rem(node, 2)


def greet(x, y, rel, node):
    barrier = pltpu.get_barrier_semaphore()

    def call(there_rel, there_node):
        pl.semaphore_signal(
            barrier, inc=1, device_id=(there_rel, there_node), device_id_type=MESH
        )

    for k in range(1, SIDE):
        call(lax.rem(x + k, SIDE) * SIDE + y, node)
        call(x * SIDE + lax.rem(y + k, SIDE), node)
    for k in range(1, NODES):
        call(rel, lax.rem(node + k, NODES))
    pl.semaphore_wait(barrier, 2 * (SIDE - 1) + NODES - 1)


def push(src, dst, send, recv, there):
    copy = pltpu.make_async_remote_copy(
        src_ref=src,
        dst_ref=dst,
        send_sem=send,
        recv_sem=recv,
        device_id=there,
        device_id_type=MESH,
    )
    copy.start()
    return copy


def gather_kernel(
    adj,
    layer,
    tiles,
    meta,
    t_all,
    a_all,
    x_all,
    m_all,
    local_sem,
    a_send,
    a_recv,
    x_send,
    x_recv,
    z_send,
    z_recv,
    t_send,
    t_recv,
    s_send,
    s_recv,
    m_send,
    m_recv,
):
    x, y, z, c, rel, node = place()
    half = ROWS // 2
    own = 1 + c
    sibling = (rel, z * 2 + (1 - c))
    beside = lax.rem(z + 7 + 2 * c, 8)
    away = 3 * (1 - c)
    quarter = quarter_of(node)

    def x_peer(k):
        return (lax.rem(x + k, SIDE) * SIDE + y, node)

    def y_peer(k):
        return (x * SIDE + lax.rem(y + k, SIDE), node)

    greet(x, y, rel, node)

    a_first = []
    for k in range(1, SIDE):
        a_first.append(
            push(
                adj.at[pl.ds(0, half)],
                a_all.at[own, x, y, pl.ds(0, half)],
                a_send.at[0, k - 1],
                a_recv.at[0, k - 1],
                x_peer(k),
            )
        )
        a_first.append(
            push(
                adj.at[pl.ds(half, half)],
                a_all.at[own, x, y, pl.ds(half, half)],
                a_send.at[1, k - 1],
                a_recv.at[1, k - 1],
                y_peer(k),
            )
        )
    a_own = pltpu.make_async_copy(adj, a_all.at[own, x, y], local_sem.at[0])
    a_own.start()

    z_copies = []
    for k in range(1, NODES):
        there = lax.rem(node + k, NODES)
        column = pl.multiple_of(quarter_of(there) * QUARTER, QUARTER)
        z_copies.append(
            push(
                layer.at[pl.ds(rel * ROWS, ROWS), pl.ds(column, QUARTER)],
                x_all.at[node, x, y],
                z_send.at[k - 1],
                z_recv.at[k - 1],
                (rel, there),
            )
        )
    x_own = pltpu.make_async_copy(
        layer.at[
            pl.ds(rel * ROWS, ROWS),
            pl.ds(pl.multiple_of(quarter * QUARTER, QUARTER), QUARTER),
        ],
        x_all.at[node, x, y],
        local_sem.at[1],
    )
    x_own.start()

    m_copies = [push(meta, m_all.at[own], m_send.at[0], m_recv.at[0], sibling)]
    m_own = pltpu.make_async_copy(meta, m_all.at[own], local_sem.at[2])
    m_own.start()
    t_far = []
    for h in range(2):
        there = (rel, beside * 2 + h)
        m_copies.append(
            push(meta, m_all.at[away], m_send.at[1 + h], m_recv.at[1 + c], there)
        )
        part = pl.ds(h * (TILES // 2), TILES // 2)
        t_far.append(
            push(
                tiles.at[part],
                t_all.at[away, part],
                t_send.at[h],
                t_recv.at[c],
                there,
            )
        )
    t_near = push(tiles, t_all.at[own], s_send.at[0], s_recv.at[0], sibling)

    def arrival(ref, sem):
        pltpu.make_async_copy(ref, ref, sem).wait()

    a_own.wait()
    for copy in a_first:
        copy.wait()
    a_second = []
    for k in range(1, SIDE):
        mine = a_all.at[own, :, y, pl.ds(0, half)]
        a_second.append(
            push(mine, mine, a_send.at[2, k - 1], a_recv.at[2, k - 1], y_peer(k))
        )
        mine = a_all.at[own, x, :, pl.ds(half, half)]
        a_second.append(
            push(mine, mine, a_send.at[3, k - 1], a_recv.at[3, k - 1], x_peer(k))
        )

    x_own.wait()
    for copy in z_copies:
        copy.wait()
    x_first = []
    for k in range(1, SIDE):
        mine = x_all.at[pl.ds(0, 8), x, y]
        x_first.append(
            push(mine, mine, x_send.at[0, k - 1], x_recv.at[0, k - 1], x_peer(k))
        )
        mine = x_all.at[pl.ds(8, 8), x, y]
        x_first.append(
            push(mine, mine, x_send.at[1, k - 1], x_recv.at[1, k - 1], y_peer(k))
        )

    for copy in a_second:
        copy.wait()
    a_far = []
    for h in range(2):
        part = pl.ds(2 * h, 2)
        a_far.append(
            push(
                a_all.at[own, part],
                a_all.at[away, part],
                t_send.at[2 + h],
                t_recv.at[2 + c],
                (rel, beside * 2 + h),
            )
        )
    a_near = push(
        a_all.at[own], a_all.at[own], s_send.at[1], s_recv.at[1], sibling
    )

    for copy in x_first:
        copy.wait()
    x_second = []
    for k in range(1, SIDE):
        mine = x_all.at[pl.ds(0, 8), :, y]
        x_second.append(
            push(mine, mine, x_send.at[2, k - 1], x_recv.at[2, k - 1], y_peer(k))
        )
        mine = x_all.at[pl.ds(8, 8), x]
        x_second.append(
            push(mine, mine, x_send.at[3, k - 1], x_recv.at[3, k - 1], x_peer(k))
        )

    onward = []
    mine = pl.ds(c * (TILES // 2), TILES // 2)
    rows = pl.ds(2 * c, 2)
    for sender, slot in ((0, 3), (1, 0)):
        arrival(t_all.at[slot, mine], t_recv.at[sender])
        onward.append(
            push(
                t_all.at[slot, mine],
                t_all.at[slot, mine],
                s_send.at[2 + sender],
                s_recv.at[2 + sender],
                sibling,
            )
        )
    for sender, slot in ((0, 3), (1, 0)):
        arrival(a_all.at[slot, rows], t_recv.at[2 + sender])
        onward.append(
            push(
                a_all.at[slot, rows],
                a_all.at[slot, rows],
                s_send.at[4 + sender],
                s_recv.at[4 + sender],
                sibling,
            )
        )

    for copy in t_far + a_far:
        copy.wait_send()
    other = 2 - c
    t_near.wait_send()
    a_near.wait_send()
    arrival(t_all.at[other], s_recv.at[0])
    arrival(a_all.at[other], s_recv.at[1])
    theirs = pl.ds((1 - c) * (TILES // 2), TILES // 2)
    their_rows = pl.ds(2 * (1 - c), 2)
    for copy in onward:
        copy.wait_send()
    for sender, slot in ((0, 3), (1, 0)):
        arrival(t_all.at[slot, theirs], s_recv.at[2 + sender])
        arrival(a_all.at[slot, their_rows], s_recv.at[4 + sender])
    for copy in m_copies:
        copy.wait_send()
    arrival(m_all.at[other], m_recv.at[0])
    arrival(m_all.at[3], m_recv.at[1])
    arrival(m_all.at[0], m_recv.at[2])
    m_own.wait()
    for copy in x_second:
        copy.wait()


def gather(adj, layer, tiles, meta):
    dma = pltpu.SemaphoreType.DMA
    return pl.pallas_call(
        gather_kernel,
        out_shape=(
            jax.ShapeDtypeStruct((4, TILES, EDGE, EDGE), jnp.bfloat16),
            jax.ShapeDtypeStruct((4, SIDE, SIDE, ROWS, FEATURE), jnp.bfloat16),
            jax.ShapeDtypeStruct((NODES, SIDE, SIDE, ROWS, QUARTER), jnp.bfloat16),
            jax.ShapeDtypeStruct((4, 8, 128), jnp.int32),
        ),
        in_specs=[ANY] * 4,
        out_specs=(ANY,) * 4,
        scratch_shapes=[
            dma((3,)),
            dma((4, 3)),
            dma((4, 3)),
            dma((4, 3)),
            dma((4, 3)),
            dma((15,)),
            dma((15,)),
            dma((4,)),
            dma((4,)),
            dma((6,)),
            dma((6,)),
            dma((3,)),
            dma((3,)),
        ],
        compiler_params=pltpu.CompilerParams(collective_id=0, has_side_effects=True),
        cost_estimate=pl.CostEstimate(
            flops=0, bytes_accessed=32 << 20, transcendentals=0
        ),
        name="gather_rows_and_tiles",
    )(adj, layer, tiles, meta)


def local_kernel(
    meta,
    own_tiles,
    tiles_in,
    a_in,
    x_in,
    weights_in,
    d_out,
    g_out,
    tiles,
    a_rows,
    x_rows,
    weights,
    d_turned,
    aw,
    d_sum,
    h_sum,
    h_turned,
    in_sem,
    tile_sem,
    out_sem,
):
    quarter = quarter_of(lax.axis_index("node"))
    shards = 4
    buckets = NODES * BLOCKS
    width = 4 * EDGE
    chunks = shards * TILES // CHUNK
    column = pl.multiple_of(quarter * QUARTER, QUARTER)

    def fetch(src, dst, sem):
        copy = pltpu.make_async_copy(src, dst, sem)
        copy.start()
        return copy

    get_w = fetch(weights_in.at[:, pl.ds(column, QUARTER)], weights, in_sem.at[0])
    get_a = [
        fetch(
            a_in.at[pl.ds(s * BLOCKS, BLOCKS)],
            a_rows.at[pl.ds(s * BLOCKS, BLOCKS)],
            in_sem.at[1 + s],
        )
        for s in range(shards)
    ]
    get_x = fetch(x_in, x_rows, in_sem.at[5])

    core = lax.rem(lax.axis_index("node"), 2)
    each = TILES // CHUNK

    def tile_copy(n):
        part = pl.ds(n * CHUNK, CHUNK)
        return pltpu.make_async_copy(tiles_in.at[part], tiles.at[part], tile_sem.at[n])

    for i in range(each):
        n = (1 + core) * each + i
        pltpu.make_async_copy(
            own_tiles.at[pl.ds(i * CHUNK, CHUNK)],
            tiles.at[pl.ds(n * CHUNK, CHUNK)],
            tile_sem.at[n],
        ).start()
        tile_copy(i).start()
        tile_copy((2 - core) * each + i).start()
        tile_copy(3 * each + i).start()

    d_sum[...] = jnp.zeros_like(d_sum)
    h_sum[...] = jnp.zeros_like(h_sum)

    get_w.wait()
    both = weights[...].reshape(2 * QUARTER, FEATURE)
    for b in range(shards * BLOCKS // 4):
        if b % 2 == 0:
            get_a[b // 2].wait()
        rows = a_rows[pl.ds(b * 4, 4)].reshape(width, FEATURE)
        value = lax.dot_general(
            both,
            rows,
            (((1,), (1,)), ((), ())),
            preferred_element_type=jnp.float32,
        ).astype(jnp.bfloat16)
        for r in range(2):
            for i in range(4):
                aw[r, b * 4 + i] = value[
                    r * QUARTER : (r + 1) * QUARTER, i * EDGE : (i + 1) * EDGE
                ]
    get_x.wait()

    def some(n, carry):
        tile_copy(n).wait()
        slot = lax.div(n * CHUNK, TILES)
        first = lax.rem(n * CHUNK, TILES)
        for k in range(CHUNK):
            code = meta[slot, 0, first + k]
            target = slot * BLOCKS + lax.rem(code, BLOCKS)
            relation = lax.rem(lax.div(code, BLOCKS), 2)
            bucket = lax.div(code, 2 * BLOCKS)
            tile = tiles[n * CHUNK + k]
            d_sum[bucket] += jnp.dot(
                aw[relation, target], tile, preferred_element_type=jnp.float32
            )
            h_sum[relation, target] += jnp.dot(
                tile, x_rows[bucket], preferred_element_type=jnp.float32
            )
        return carry

    lax.fori_loop(0, chunks, some, 0)

    def out_copy(n):
        part = pl.ds(n * 16, 16)
        return pltpu.make_async_copy(d_turned.at[part], d_out.at[part], out_sem.at[n])

    def turn(n, carry):
        for k in range(16):
            d_turned[n * 16 + k] = d_sum[n * 16 + k].astype(jnp.bfloat16).T
        out_copy(n).start()
        return carry

    lax.fori_loop(0, buckets // 16, turn, 0)
    for r in range(2):
        for b in range(shards * BLOCKS):
            h_turned[:, pl.ds(b * EDGE, EDGE)] = h_sum[r, b].astype(jnp.bfloat16).T
        g_out[r] = jnp.dot(
            h_turned[...],
            a_rows[...].reshape(shards * BLOCKS * EDGE, FEATURE),
            preferred_element_type=jnp.float32,
        )
    for n in range(buckets // 16):
        out_copy(n).wait()


def local(meta, own_tiles, tiles, a_rows, x_rows, weights):
    buckets = NODES * BLOCKS
    shards = 4
    bf16 = jnp.bfloat16
    return pl.pallas_call(
        local_kernel,
        out_shape=(
            jax.ShapeDtypeStruct((buckets, EDGE, QUARTER), bf16),
            jax.ShapeDtypeStruct((2, QUARTER, FEATURE), jnp.float32),
        ),
        in_specs=[SMEM, ANY, ANY, ANY, ANY, ANY],
        out_specs=(ANY, VMEM),
        scratch_shapes=[
            pltpu.VMEM((shards * TILES, EDGE, EDGE), bf16),
            pltpu.VMEM((shards * BLOCKS, EDGE, FEATURE), bf16),
            pltpu.VMEM((buckets, EDGE, QUARTER), bf16),
            pltpu.VMEM((2, QUARTER, FEATURE), bf16),
            pltpu.VMEM((buckets, EDGE, QUARTER), bf16),
            pltpu.VMEM((2, shards * BLOCKS, QUARTER, EDGE), bf16),
            pltpu.VMEM((buckets, QUARTER, EDGE), jnp.float32),
            pltpu.VMEM((2, shards * BLOCKS, EDGE, QUARTER), jnp.float32),
            pltpu.VMEM((QUARTER, shards * BLOCKS * EDGE), bf16),
            pltpu.SemaphoreType.DMA((6,)),
            pltpu.SemaphoreType.DMA((shards * TILES // CHUNK,)),
            pltpu.SemaphoreType.DMA((buckets // 16,)),
        ],
        compiler_params=pltpu.CompilerParams(vmem_limit_bytes=56 << 20),
        name="tile_products",
    )(meta, own_tiles, tiles, a_rows, x_rows, weights)


def reduce_kernel(
    d_part,
    g_part,
    adj,
    self_weight,
    g_out,
    d_out,
    own_a,
    own_b,
    got_a,
    got_b,
    sum_a,
    sum_b,
    next_a,
    next_b,
    total,
    got_z,
    got_g,
    own_term,
    local_sem,
    a_send,
    a_recv,
    z_send,
    z_recv,
    g_send,
    g_recv,
):
    x, y, z, c, rel, node = place()
    quarter = quarter_of(node)
    half = NODES // 2

    def x_peer(k):
        return (lax.rem(x + k, SIDE) * SIDE + y, node)

    def y_peer(k):
        return (x * SIDE + lax.rem(y + k, SIDE), node)

    greet(x, y, rel, node)

    first = []
    for k in range(1, SIDE):
        first.append(
            push(
                d_part.at[pl.ds(0, half), lax.rem(x + k, SIDE)],
                got_a.at[k - 1],
                a_send.at[0, k - 1],
                a_recv.at[0, k - 1],
                x_peer(k),
            )
        )
        first.append(
            push(
                d_part.at[pl.ds(half, half), :, lax.rem(y + k, SIDE)],
                got_b.at[k - 1],
                a_send.at[1, k - 1],
                a_recv.at[1, k - 1],
                y_peer(k),
            )
        )
    mine_a = pltpu.make_async_copy(
        d_part.at[pl.ds(0, half), x], own_a, local_sem.at[0]
    )
    mine_a.start()
    mine_b = pltpu.make_async_copy(
        d_part.at[pl.ds(half, half), :, y], own_b, local_sem.at[1]
    )
    mine_b.start()

    sender = lax.div(z, 2)
    for m in range(4):
        owner = quarter * 4 + m
        rows = g_part.at[:, pl.ds(32 * m, 32), :]

        @pl.when(owner != node)
        def _():
            push(
                rows,
                got_g.at[sender],
                g_send.at[m],
                g_recv.at[sender],
                (rel, owner),
            )

        @pl.when(owner == node)
        def _():
            pltpu.make_async_copy(rows, got_g.at[sender], g_recv.at[sender]).start()

    own_term[...] = lax.dot_general(
        adj[...],
        self_weight[...],
        (((1,), (1,)), ((), ())),
        preferred_element_type=jnp.float32,
    )

    mine_a.wait()
    mine_b.wait()
    for copy in first:
        copy.wait()

    def f32(value):
        return value.astype(jnp.float32)

    def add_first(n, carry):
        for own, got, into in ((own_a, got_a, sum_a), (own_b, got_b, sum_b)):
            value = f32(own[n])
            for k in range(SIDE - 1):
                value = value + f32(got[k, n])
            into[n] = value.astype(jnp.bfloat16)
        return carry

    lax.fori_loop(0, half, add_first, 0)

    second = []
    for k in range(1, SIDE):
        second.append(
            push(
                sum_a.at[:, lax.rem(y + k, SIDE)],
                next_a.at[k - 1],
                a_send.at[2, k - 1],
                a_recv.at[2, k - 1],
                y_peer(k),
            )
        )
        second.append(
            push(
                sum_b.at[:, lax.rem(x + k, SIDE)],
                next_b.at[k - 1],
                a_send.at[3, k - 1],
                a_recv.at[3, k - 1],
                x_peer(k),
            )
        )

    for m in range(4):
        pltpu.make_async_copy(got_g.at[m], got_g.at[m], g_recv.at[m]).wait()
        owner = quarter * 4 + m
        rows = g_part.at[:, pl.ds(32 * m, 32), :]

        @pl.when(owner != node)
        def _():
            pltpu.make_async_remote_copy(
                src_ref=rows,
                dst_ref=got_g.at[sender],
                send_sem=g_send.at[m],
                recv_sem=g_recv.at[sender],
                device_id=(rel, owner),
                device_id_type=MESH,
            ).wait_send()

    g_out[...] = (got_g[0] + got_g[1]) + (got_g[2] + got_g[3])

    for copy in second:
        copy.wait()

    def add_second(n, carry):
        for own, at, got, base in (
            (sum_a, y, next_a, 0),
            (sum_b, x, next_b, half),
        ):
            value = f32(own[n, at])
            for k in range(SIDE - 1):
                value = value + f32(got[k, n])
            total[base + n] = value.astype(jnp.bfloat16)
        return carry

    lax.fori_loop(0, half, add_second, 0)

    z_copies = []
    for k in range(1, NODES):
        there = lax.rem(node + k, NODES)
        z_copies.append(
            push(
                total.at[there],
                got_z.at[node],
                z_send.at[k - 1],
                z_recv.at[k - 1],
                (rel, there),
            )
        )
    mine_z = pltpu.make_async_copy(total.at[node], got_z.at[node], local_sem.at[2])
    mine_z.start()
    mine_z.wait()
    for copy in z_copies:
        copy.wait()
    for q in range(4):
        columns = pl.ds(q * QUARTER, QUARTER)
        value = own_term[:, columns]
        for step in range(4):
            value = value + f32(got_z[(2 * step + q // 2) * 2 + q % 2])
        d_out[:, columns] = value.astype(jnp.bfloat16)


def reduce(d_part, g_part, adj, self_weight):
    dma = pltpu.SemaphoreType.DMA
    half = NODES // 2
    bf16 = jnp.bfloat16
    return pl.pallas_call(
        reduce_kernel,
        out_shape=(
            jax.ShapeDtypeStruct((2, 32, FEATURE), jnp.float32),
            jax.ShapeDtypeStruct((ROWS, FEATURE), bf16),
        ),
        in_specs=[ANY, ANY, VMEM, VMEM],
        out_specs=(VMEM, VMEM),
        scratch_shapes=[
            pltpu.VMEM((half, SIDE, ROWS, QUARTER), bf16),
            pltpu.VMEM((half, SIDE, ROWS, QUARTER), bf16),
            pltpu.VMEM((3, half, SIDE, ROWS, QUARTER), bf16),
            pltpu.VMEM((3, half, SIDE, ROWS, QUARTER), bf16),
            pltpu.VMEM((half, SIDE, ROWS, QUARTER), bf16),
            pltpu.VMEM((half, SIDE, ROWS, QUARTER), bf16),
            pltpu.VMEM((3, half, ROWS, QUARTER), bf16),
            pltpu.VMEM((3, half, ROWS, QUARTER), bf16),
            pltpu.VMEM((NODES, ROWS, QUARTER), bf16),
            pltpu.VMEM((NODES, ROWS, QUARTER), bf16),
            pltpu.VMEM((4, 2, 32, FEATURE), jnp.float32),
            pltpu.VMEM((ROWS, FEATURE), jnp.float32),
            dma((3,)),
            dma((4, 3)),
            dma((4, 3)),
            dma((15,)),
            dma((15,)),
            dma((4,)),
            dma((4,)),
        ],
        compiler_params=pltpu.CompilerParams(
            collective_id=1, has_side_effects=True, vmem_limit_bytes=32 << 20
        ),
        name="sum_terms",
    )(d_part, g_part, adj, self_weight)


def on_device(
    out_adjoint,
    layer_input,
    rel_weights,
    self_weight,
    tile_values,
    tile_rel,
    tile_target,
    tile_src,
    tile_dest,
):
    code = (
        (tile_dest[:, :, 0] * BLOCKS + tile_src) * 2 + tile_rel
    ) * BLOCKS + tile_target
    meta = jnp.pad(code, ((0, 7), (0, 128 - TILES)))
    adj = out_adjoint[0]
    tiles, a_rows, x_rows, codes = gather(adj, layer_input[0], tile_values[0], meta)
    d_part, g_part = local(
        codes,
        tile_values[0],
        tiles.reshape(4 * TILES, EDGE, EDGE),
        a_rows.reshape(4 * BLOCKS, EDGE, FEATURE),
        x_rows.reshape(NODES * BLOCKS, EDGE, QUARTER),
        rel_weights,
    )
    rel_weight_grad, d_source = reduce(
        d_part.reshape(NODES, SIDE, SIDE, ROWS, QUARTER), g_part, adj, self_weight
    )
    return rel_weight_grad, d_source[None]


def solution(mesh):
    return jax.shard_map(
        on_device,
        mesh=mesh,
        in_specs=(
            P("node", "rel", None),
            P("node", None, None),
            P("rel", None, None),
            P(),
            P("rel", "node", None, None),
            P("rel", "node"),
            P("rel", "node"),
            P("rel", "node"),
            P("rel", "node", None),
        ),
        out_specs=(P("rel", "node", None), P("node", "rel", None)),
        check_vma=False,
    )
```

```python
import jax
import jax.numpy as jnp
from jax import lax
from jax.experimental import pallas as pl
from jax.experimental.pallas import tpu as pltpu
from jax.sharding import PartitionSpec as P

MESH = pl.DeviceIdType.MESH
ANY = pl.BlockSpec(memory_space=pl.ANY)
VMEM = pl.BlockSpec(memory_space=pltpu.VMEM)
SMEM = pl.BlockSpec(memory_space=pltpu.SMEM)

SIDE = 4
NODES = 16
ROWS = 64
QUARTER = 128
TILES = 64
EDGE = 128
FEATURE = 512
BLOCKS = 8
CHUNK = 32


def place():
    rel, node = lax.axis_index("rel"), lax.axis_index("node")
    return (
        lax.div(rel, SIDE),
        lax.rem(rel, SIDE),
        lax.div(node, 2),
        lax.rem(node, 2),
        rel,
        node,
    )


def quarter_of(node):
    return lax.rem(lax.div(node, 2), 2) * 2 + lax.rem(node, 2)


def greet(x, y, rel, node):
    barrier = pltpu.get_barrier_semaphore()

    def call(there):
        pl.semaphore_signal(barrier, inc=1, device_id=there, device_id_type=MESH)

    for k in range(1, SIDE):
        call((lax.rem(x + k, SIDE) * SIDE + y, node))
        call((x * SIDE + lax.rem(y + k, SIDE), node))
    for k in range(1, NODES):
        call((rel, lax.rem(node + k, NODES)))
    pl.semaphore_wait(barrier, 2 * (SIDE - 1) + NODES - 1)


def push(src, dst, send, recv, there):
    copy = pltpu.make_async_remote_copy(
        src_ref=src,
        dst_ref=dst,
        send_sem=send,
        recv_sem=recv,
        device_id=there,
        device_id_type=MESH,
    )
    copy.start()
    return copy


def arrival(ref, sem):
    pltpu.make_async_copy(ref, ref, sem).wait()


class RingGather:
    def __init__(self, block, at, peer, send, recv):
        self.block, self.at, self.peer, self.send, self.recv = (
            block,
            at,
            peer,
            send,
            recv,
        )
        self.copies = []

    def move(self, view, number, k):
        self.copies.append(
            push(
                view,
                view,
                self.send.at[number],
                self.recv.at[number],
                self.peer(k),
            )
        )

    def place(self, k):
        return lax.rem(self.at + k, SIDE)

    def begin(self):
        mine = self.block(self.at, None)
        self.move(mine, 0, 1)
        self.move(mine, 1, SIDE - 1)

    def forward(self):
        arrival(self.block(self.place(3), None), self.recv.at[0])
        self.move(self.block(self.place(3), 0), 2, 1)
        arrival(self.block(self.place(1), None), self.recv.at[1])
        self.move(self.block(self.place(1), 1), 3, SIDE - 1)

    def finish(self):
        arrival(self.block(self.place(2), 0), self.recv.at[2])
        arrival(self.block(self.place(2), 1), self.recv.at[3])

    def sent(self):
        for copy in self.copies:
            copy.wait_send()


def gather_kernel(
    adj,
    layer,
    tiles,
    meta,
    t_all,
    a_all,
    x_all,
    m_all,
    local_sem,
    f_send,
    f_recv,
    a_send,
    a_recv,
    x_send,
    x_recv,
    z_send,
    z_recv,
    t_send,
    t_recv,
    s_send,
    s_recv,
    m_send,
    m_recv,
):
    x, y, z, c, rel, node = place()
    half = ROWS // 2
    own = 1 + c
    near = 3 * c
    other = 2 - c
    sibling = (rel, z * 2 + (1 - c))
    beside = lax.rem(z + 7 + 2 * c, 8)
    away = 3 * (1 - c)
    quarter = quarter_of(node)
    halves = TILES // 2

    def x_peer(k):
        return (lax.rem(x + k, SIDE) * SIDE + y, node)

    def y_peer(k):
        return (x * SIDE + lax.rem(y + k, SIDE), node)

    def a_view(px, py, rows, h):
        slots = pl.ds(2 * c, 2) if h is None else 2 * c + h
        return a_all.at[slots, px, py, rows]

    every = slice(None)
    low, high = pl.ds(0, half), pl.ds(half, half)
    a_rings = (
        RingGather(
            lambda p, h: a_view(every, p, low, h), y, y_peer, a_send.at[0], a_recv.at[0]
        ),
        RingGather(
            lambda p, h: a_view(p, every, high, h), x, x_peer, a_send.at[1], a_recv.at[1]
        ),
    )

    def x_view(stream, px, py, h):
        shards = pl.ds(4 * stream, 4) if h is None else pl.ds(4 * stream + 2 * h, 2)
        return x_all.at[shards, px, py]

    def x_ring(stream, leg):
        number = 2 * stream + leg
        along_x = (stream + leg) % 2 == 0
        if along_x:
            others = y if leg == 0 else every
            return RingGather(
                lambda p, h: x_view(stream, p, others, h),
                x,
                x_peer,
                x_send.at[number],
                x_recv.at[number],
            )
        others = x if leg == 0 else every
        return RingGather(
            lambda p, h: x_view(stream, others, p, h),
            y,
            y_peer,
            x_send.at[number],
            x_recv.at[number],
        )

    x_rings = [[x_ring(stream, leg) for leg in range(2)] for stream in range(4)]

    greet(x, y, rel, node)

    a_near = push(
        adj,
        a_all.at[away, x, y],
        t_send.at[2],
        t_recv.at[2],
        (rel, beside * 2 + 1 - c),
    )

    a_first = []

    def a_send_first(source, slot, number):
        for k in range(1, SIDE):
            for rows, peer, stream in ((low, x_peer, 0), (high, y_peer, 1)):
                at = (number, stream, k - 1)
                a_first.append(
                    push(
                        source.at[rows],
                        a_all.at[slot, x, y, rows],
                        f_send.at[at],
                        f_recv.at[at],
                        peer(k),
                    )
                )

    a_send_first(adj, own, 0)
    a_own = pltpu.make_async_copy(adj, a_all.at[own, x, y], local_sem.at[0])
    a_own.start()

    z_copies = []
    for k in range(1, NODES):
        there = lax.rem(node + k, NODES)
        column = pl.multiple_of(quarter_of(there) * QUARTER, QUARTER)
        z_copies.append(
            push(
                layer.at[pl.ds(rel * ROWS, ROWS), pl.ds(column, QUARTER)],
                x_all.at[node, x, y],
                z_send.at[k - 1],
                z_recv.at[k - 1],
                (rel, there),
            )
        )
    x_own = pltpu.make_async_copy(
        layer.at[
            pl.ds(rel * ROWS, ROWS),
            pl.ds(pl.multiple_of(quarter * QUARTER, QUARTER), QUARTER),
        ],
        x_all.at[node, x, y],
        local_sem.at[1],
    )
    x_own.start()

    arrival(a_all.at[near, x, y], t_recv.at[2])
    a_send_first(a_all.at[near, x, y], near, 1)

    t_near = push(tiles, t_all.at[own], s_send.at[0], s_recv.at[0], sibling)
    m_copies = [push(meta, m_all.at[own], m_send.at[0], m_recv.at[0], sibling)]
    for h in range(2):
        m_copies.append(
            push(
                meta,
                m_all.at[away],
                m_send.at[1 + h],
                m_recv.at[1 + c],
                (rel, beside * 2 + h),
            )
        )
    m_own = pltpu.make_async_copy(meta, m_all.at[own], local_sem.at[2])
    m_own.start()

    a_own.wait()
    for copy in a_first:
        copy.wait_recv()
    for ring in a_rings:
        ring.begin()

    x_own.wait()
    for copy in z_copies:
        copy.wait_recv()
    for stream in range(4):
        x_rings[stream][0].begin()
    t_far = []
    for h in range(2):
        part = pl.ds(h * halves, halves)
        t_far.append(
            push(
                tiles.at[part],
                t_all.at[away, part],
                t_send.at[h],
                t_recv.at[c],
                (rel, beside * 2 + h),
            )
        )
    for ring in a_rings:
        ring.forward()
    for stream in range(4):
        x_rings[stream][0].forward()
    for stream in range(4):
        x_rings[stream][0].finish()
        x_rings[stream][1].begin()
    for ring in a_rings:
        ring.finish()
    pair = pl.ds(2 * c, 2)
    a_over = push(a_all.at[pair], a_all.at[pair], s_send.at[1], s_recv.at[1], sibling)
    for stream in range(4):
        x_rings[stream][1].forward()

    onward = []
    mine = pl.ds(c * halves, halves)
    for sender, slot in ((0, 3), (1, 0)):
        arrival(t_all.at[slot, mine], t_recv.at[sender])
        onward.append(
            push(
                t_all.at[slot, mine],
                t_all.at[slot, mine],
                s_send.at[2 + sender],
                s_recv.at[2 + sender],
                sibling,
            )
        )
    for stream in range(4):
        x_rings[stream][1].finish()

    arrival(t_all.at[other], s_recv.at[0])
    arrival(a_all.at[pl.ds(2 - 2 * c, 2)], s_recv.at[1])
    theirs = pl.ds((1 - c) * halves, halves)
    for sender, slot in ((0, 3), (1, 0)):
        arrival(t_all.at[slot, theirs], s_recv.at[2 + sender])
    arrival(m_all.at[other], m_recv.at[0])
    arrival(m_all.at[3], m_recv.at[1])
    arrival(m_all.at[0], m_recv.at[2])
    m_own.wait()
    for ring in a_rings:
        ring.sent()
    for rings in x_rings:
        for ring in rings:
            ring.sent()
    for copy in [a_near, t_near, a_over] + a_first + z_copies + m_copies + t_far + onward:
        copy.wait_send()


def gather(adj, layer, tiles, meta):
    dma = pltpu.SemaphoreType.DMA
    return pl.pallas_call(
        gather_kernel,
        out_shape=(
            jax.ShapeDtypeStruct((4, TILES, EDGE, EDGE), jnp.bfloat16),
            jax.ShapeDtypeStruct((4, SIDE, SIDE, ROWS, FEATURE), jnp.bfloat16),
            jax.ShapeDtypeStruct((NODES, SIDE, SIDE, ROWS, QUARTER), jnp.bfloat16),
            jax.ShapeDtypeStruct((4, 8, 128), jnp.int32),
        ),
        in_specs=[ANY] * 4,
        out_specs=(ANY,) * 4,
        scratch_shapes=[
            dma((3,)),
            dma((2, 2, 3)),
            dma((2, 2, 3)),
            dma((2, 4)),
            dma((2, 4)),
            dma((8, 4)),
            dma((8, 4)),
            dma((15,)),
            dma((15,)),
            dma((3,)),
            dma((3,)),
            dma((4,)),
            dma((4,)),
            dma((3,)),
            dma((3,)),
        ],
        compiler_params=pltpu.CompilerParams(collective_id=0, has_side_effects=True),
        cost_estimate=pl.CostEstimate(
            flops=0, bytes_accessed=32 << 20, transcendentals=0
        ),
        name="gather_rows_and_tiles",
    )(adj, layer, tiles, meta)


def local_kernel(
    meta,
    own_tiles,
    tiles_in,
    a_in,
    x_in,
    weights_in,
    d_out,
    g_out,
    tiles,
    a_rows,
    x_rows,
    weights,
    d_turned,
    aw,
    d_sum,
    h_sum,
    h_turned,
    in_sem,
    tile_sem,
    out_sem,
):
    quarter = quarter_of(lax.axis_index("node"))
    shards = 4
    buckets = NODES * BLOCKS
    width = 4 * EDGE
    chunks = shards * TILES // CHUNK
    column = pl.multiple_of(quarter * QUARTER, QUARTER)

    def fetch(src, dst, sem):
        copy = pltpu.make_async_copy(src, dst, sem)
        copy.start()
        return copy

    get_w = fetch(weights_in.at[:, pl.ds(column, QUARTER)], weights, in_sem.at[0])
    get_a = [
        fetch(
            a_in.at[pl.ds(s * BLOCKS, BLOCKS)],
            a_rows.at[pl.ds(s * BLOCKS, BLOCKS)],
            in_sem.at[1 + s],
        )
        for s in range(shards)
    ]
    get_x = fetch(x_in, x_rows, in_sem.at[5])

    core = lax.rem(lax.axis_index("node"), 2)
    each = TILES // CHUNK

    def tile_copy(n):
        part = pl.ds(n * CHUNK, CHUNK)
        return pltpu.make_async_copy(tiles_in.at[part], tiles.at[part], tile_sem.at[n])

    for i in range(each):
        n = (1 + core) * each + i
        pltpu.make_async_copy(
            own_tiles.at[pl.ds(i * CHUNK, CHUNK)],
            tiles.at[pl.ds(n * CHUNK, CHUNK)],
            tile_sem.at[n],
        ).start()
        tile_copy(i).start()
        tile_copy((2 - core) * each + i).start()
        tile_copy(3 * each + i).start()

    d_sum[...] = jnp.zeros_like(d_sum)
    h_sum[...] = jnp.zeros_like(h_sum)

    get_w.wait()
    both = weights[...].reshape(2 * QUARTER, FEATURE)
    for b in range(shards * BLOCKS // 4):
        if b % 2 == 0:
            get_a[b // 2].wait()
        rows = a_rows[pl.ds(b * 4, 4)].reshape(width, FEATURE)
        value = lax.dot_general(
            both,
            rows,
            (((1,), (1,)), ((), ())),
            preferred_element_type=jnp.float32,
        ).astype(jnp.bfloat16)
        for r in range(2):
            for i in range(4):
                aw[r, b * 4 + i] = value[
                    r * QUARTER : (r + 1) * QUARTER, i * EDGE : (i + 1) * EDGE
                ]
    get_x.wait()

    def some(n, carry):
        tile_copy(n).wait()
        slot = lax.div(n * CHUNK, TILES)
        first = lax.rem(n * CHUNK, TILES)
        for k in range(CHUNK):
            code = meta[slot, 0, first + k]
            target = slot * BLOCKS + lax.rem(code, BLOCKS)
            relation = lax.rem(lax.div(code, BLOCKS), 2)
            bucket = lax.div(code, 2 * BLOCKS)
            tile = tiles[n * CHUNK + k]
            d_sum[bucket] += jnp.dot(
                aw[relation, target], tile, preferred_element_type=jnp.float32
            )
            h_sum[relation, target] += jnp.dot(
                tile, x_rows[bucket], preferred_element_type=jnp.float32
            )
        return carry

    lax.fori_loop(0, chunks, some, 0)

    def out_copy(n):
        part = pl.ds(n * 16, 16)
        return pltpu.make_async_copy(d_turned.at[part], d_out.at[part], out_sem.at[n])

    def turn(n, carry):
        for k in range(16):
            d_turned[n * 16 + k] = d_sum[n * 16 + k].astype(jnp.bfloat16).T
        out_copy(n).start()
        return carry

    lax.fori_loop(0, buckets // 16, turn, 0)
    for r in range(2):
        for b in range(shards * BLOCKS):
            h_turned[:, pl.ds(b * EDGE, EDGE)] = h_sum[r, b].astype(jnp.bfloat16).T
        g_out[r] = jnp.dot(
            h_turned[...],
            a_rows[...].reshape(shards * BLOCKS * EDGE, FEATURE),
            preferred_element_type=jnp.float32,
        )
    for n in range(buckets // 16):
        out_copy(n).wait()


def local(meta, own_tiles, tiles, a_rows, x_rows, weights):
    buckets = NODES * BLOCKS
    shards = 4
    bf16 = jnp.bfloat16
    return pl.pallas_call(
        local_kernel,
        out_shape=(
            jax.ShapeDtypeStruct((buckets, EDGE, QUARTER), bf16),
            jax.ShapeDtypeStruct((2, QUARTER, FEATURE), jnp.float32),
        ),
        in_specs=[SMEM, ANY, ANY, ANY, ANY, ANY],
        out_specs=(ANY, VMEM),
        scratch_shapes=[
            pltpu.VMEM((shards * TILES, EDGE, EDGE), bf16),
            pltpu.VMEM((shards * BLOCKS, EDGE, FEATURE), bf16),
            pltpu.VMEM((buckets, EDGE, QUARTER), bf16),
            pltpu.VMEM((2, QUARTER, FEATURE), bf16),
            pltpu.VMEM((buckets, EDGE, QUARTER), bf16),
            pltpu.VMEM((2, shards * BLOCKS, QUARTER, EDGE), bf16),
            pltpu.VMEM((buckets, QUARTER, EDGE), jnp.float32),
            pltpu.VMEM((2, shards * BLOCKS, EDGE, QUARTER), jnp.float32),
            pltpu.VMEM((QUARTER, shards * BLOCKS * EDGE), bf16),
            pltpu.SemaphoreType.DMA((6,)),
            pltpu.SemaphoreType.DMA((shards * TILES // CHUNK,)),
            pltpu.SemaphoreType.DMA((buckets // 16,)),
        ],
        compiler_params=pltpu.CompilerParams(vmem_limit_bytes=40 << 20),
        name="tile_products",
    )(meta, own_tiles, tiles, a_rows, x_rows, weights)


class RingSum:
    def __init__(self, term, send_term, at, peer, got, out, send, recv):
        self.term, self.send_term, self.at, self.peer = term, send_term, at, peer
        self.got, self.out, self.send, self.recv = got, out, send, recv
        self.copies = []

    def place(self, k):
        return lax.rem(self.at + k, SIDE)

    def move(self, view, number, k):
        self.copies.append(
            push(
                view,
                self.got.at[number],
                self.send.at[number],
                self.recv.at[number],
                self.peer(k),
            )
        )

    def begin(self):
        self.move(self.send_term(self.place(2), 0), 0, SIDE - 1)
        self.move(self.send_term(self.place(2), 1), 1, 1)

    def direct(self):
        self.move(self.send_term(self.place(1), 0), 2, 1)
        self.move(self.send_term(self.place(3), 1), 3, SIDE - 1)

    def pass_on(self):
        for number, k, h in ((0, SIDE - 1, 0), (1, 1, 1)):
            arrival(self.got.at[number], self.recv.at[number])
            value = f32(self.term(self.place(k), h)[...]) + f32(self.got[number])
            self.out[h] = value.astype(jnp.bfloat16)
            self.move(self.out.at[h], 4 + h, k)

    def result(self, h):
        for number in (2 + h, 4 + h):
            arrival(self.got.at[number], self.recv.at[number])
        value = f32(self.got[2 + h]) + f32(self.got[4 + h])
        return (value + f32(self.term(self.at, h)[...])).astype(jnp.bfloat16)

    def sent(self):
        for copy in self.copies:
            copy.wait_send()


def f32(value):
    return value.astype(jnp.float32)


def reduce_kernel(
    d_part,
    g_part,
    adj_in,
    self_weight_in,
    g_out,
    d_out,
    d_here,
    got_first,
    out_first,
    got_second,
    out_second,
    summed,
    total,
    got_z,
    got_g,
    adj,
    self_weight,
    local_sem,
    d_sem,
    r_send,
    r_recv,
    z_send,
    z_recv,
    g_send,
    g_recv,
):
    x, y, z, c, rel, node = place()
    quarter = quarter_of(node)
    streams = 4

    def x_peer(k):
        return (lax.rem(x + k, SIDE) * SIDE + y, node)

    def y_peer(k):
        return (x * SIDE + lax.rem(y + k, SIDE), node)

    def fetch(src, dst, sem):
        copy = pltpu.make_async_copy(src, dst, sem)
        copy.start()
        return copy

    get_d = []
    for stream in range(streams):
        part = pl.ds(4 * stream, 4)
        get_d.append(fetch(d_part.at[part], d_here.at[part], d_sem.at[stream]))
    get_adj = fetch(adj_in, adj, local_sem.at[0])
    get_weight = fetch(self_weight_in, self_weight, local_sem.at[1])

    def first_ring(stream):
        along_x = stream % 2 == 0

        def view(ref, p, h):
            shards = pl.ds(4 * stream + 2 * h, 2)
            return ref.at[shards, p] if along_x else ref.at[shards, :, p]

        return RingSum(
            lambda p, h: view(d_here, p, h),
            lambda p, h: view(d_part, p, h),
            x if along_x else y,
            x_peer if along_x else y_peer,
            got_first.at[stream],
            out_first.at[stream],
            r_send.at[2 * stream],
            r_recv.at[2 * stream],
        )

    def second_ring(stream):
        along_x = stream % 2 == 1

        def view(p, h):
            return summed.at[stream, pl.ds(2 * h, 2), p]

        return RingSum(
            view,
            view,
            x if along_x else y,
            x_peer if along_x else y_peer,
            got_second.at[stream],
            out_second.at[stream],
            r_send.at[2 * stream + 1],
            r_recv.at[2 * stream + 1],
        )

    firsts = [first_ring(stream) for stream in range(streams)]
    seconds = [second_ring(stream) for stream in range(streams)]

    greet(x, y, rel, node)

    for ring in firsts:
        ring.begin()
    for ring in firsts[:2]:
        ring.direct()

    sender = lax.div(z, 2)
    for m in range(4):
        owner = quarter * 4 + m
        rows = g_part.at[:, pl.ds(32 * m, 32), :]

        @pl.when(owner != node)
        def _():
            push(
                rows,
                got_g.at[sender],
                g_send.at[m],
                g_recv.at[sender],
                (rel, owner),
            )

        @pl.when(owner == node)
        def _():
            pltpu.make_async_copy(rows, got_g.at[sender], g_recv.at[sender]).start()

    def middle(stream):
        for h in range(2):
            summed[stream, pl.ds(2 * h, 2)] = firsts[stream].result(h)
        seconds[stream].begin()
        seconds[stream].direct()

    def last(stream):
        for h in range(2):
            total[pl.ds(4 * stream + 2 * h, 2)] = seconds[stream].result(h)
        for n in range(4 * stream, 4 * stream + 4):

            @pl.when(node != n)
            def _():
                push(
                    total.at[n],
                    got_z.at[node],
                    z_send.at[n],
                    z_recv.at[node],
                    (rel, n),
                )

            @pl.when(node == n)
            def _():
                pltpu.make_async_copy(
                    total.at[n], got_z.at[node], z_recv.at[node]
                ).start()

    for stream in range(streams):
        get_d[stream].wait()
    for ring in firsts[:2]:
        ring.pass_on()
    for ring in firsts[2:]:
        ring.direct()
    for ring in firsts[2:]:
        ring.pass_on()
    middle(0)
    middle(1)
    seconds[0].pass_on()
    seconds[1].pass_on()
    middle(2)
    middle(3)
    last(0)
    last(1)
    seconds[2].pass_on()
    seconds[3].pass_on()
    last(2)
    last(3)

    get_adj.wait()
    get_weight.wait()
    own_term = lax.dot_general(
        adj[...],
        self_weight[...],
        (((1,), (1,)), ((), ())),
        preferred_element_type=jnp.float32,
    )

    for m in range(4):
        arrival(got_g.at[m], g_recv.at[m])
    g_out[...] = (got_g[0] + got_g[1]) + (got_g[2] + got_g[3])

    for n in range(NODES):
        arrival(got_z.at[n], z_recv.at[n])
    for q in range(4):
        value = own_term[:, q * QUARTER : (q + 1) * QUARTER]
        for step in range(4):
            value = value + f32(got_z[(2 * step + q // 2) * 2 + q % 2])
        d_out[:, q * QUARTER : (q + 1) * QUARTER] = value.astype(jnp.bfloat16)

    for ring in firsts + seconds:
        ring.sent()
    for m in range(4):
        owner = quarter * 4 + m

        @pl.when(owner != node)
        def _():
            pltpu.make_async_remote_copy(
                src_ref=g_part.at[:, pl.ds(32 * m, 32), :],
                dst_ref=got_g.at[sender],
                send_sem=g_send.at[m],
                recv_sem=g_recv.at[sender],
                device_id=(rel, owner),
                device_id_type=MESH,
            ).wait_send()

    for n in range(NODES):

        @pl.when(node != n)
        def _():
            pltpu.make_async_remote_copy(
                src_ref=total.at[n],
                dst_ref=got_z.at[node],
                send_sem=z_send.at[n],
                recv_sem=z_recv.at[node],
                device_id=(rel, n),
                device_id_type=MESH,
            ).wait_send()


def reduce(d_part, g_part, adj, self_weight):
    dma = pltpu.SemaphoreType.DMA
    bf16 = jnp.bfloat16
    return pl.pallas_call(
        reduce_kernel,
        out_shape=(
            jax.ShapeDtypeStruct((2, 32, FEATURE), jnp.float32),
            jax.ShapeDtypeStruct((ROWS, FEATURE), bf16),
        ),
        in_specs=[ANY, ANY, ANY, ANY],
        out_specs=(VMEM, VMEM),
        scratch_shapes=[
            pltpu.VMEM((NODES, SIDE, SIDE, ROWS, QUARTER), bf16),
            pltpu.VMEM((4, 6, 2, SIDE, ROWS, QUARTER), bf16),
            pltpu.VMEM((4, 2, 2, SIDE, ROWS, QUARTER), bf16),
            pltpu.VMEM((4, 6, 2, ROWS, QUARTER), bf16),
            pltpu.VMEM((4, 2, 2, ROWS, QUARTER), bf16),
            pltpu.VMEM((4, 4, SIDE, ROWS, QUARTER), bf16),
            pltpu.VMEM((NODES, ROWS, QUARTER), bf16),
            pltpu.VMEM((NODES, ROWS, QUARTER), bf16),
            pltpu.VMEM((4, 2, 32, FEATURE), jnp.float32),
            pltpu.VMEM((ROWS, FEATURE), bf16),
            pltpu.VMEM((FEATURE, FEATURE), bf16),
            dma((2,)),
            dma((4,)),
            dma((8, 6)),
            dma((8, 6)),
            dma((16,)),
            dma((16,)),
            dma((4,)),
            dma((4,)),
        ],
        compiler_params=pltpu.CompilerParams(
            collective_id=1, has_side_effects=True, vmem_limit_bytes=24 << 20
        ),
        name="sum_terms",
    )(d_part, g_part, adj, self_weight)


def on_device(
    out_adjoint,
    layer_input,
    rel_weights,
    self_weight,
    tile_values,
    tile_rel,
    tile_target,
    tile_src,
    tile_dest,
):
    code = (
        (tile_dest[:, :, 0] * BLOCKS + tile_src) * 2 + tile_rel
    ) * BLOCKS + tile_target
    meta = jnp.pad(code, ((0, 7), (0, 128 - TILES)))
    adj = out_adjoint[0]
    tiles, a_rows, x_rows, codes = gather(adj, layer_input[0], tile_values[0], meta)
    d_part, g_part = local(
        codes,
        tile_values[0],
        tiles.reshape(4 * TILES, EDGE, EDGE),
        a_rows.reshape(4 * BLOCKS, EDGE, FEATURE),
        x_rows.reshape(NODES * BLOCKS, EDGE, QUARTER),
        rel_weights,
    )
    rel_weight_grad, d_source = reduce(
        d_part.reshape(NODES, SIDE, SIDE, ROWS, QUARTER), g_part, adj, self_weight
    )
    return rel_weight_grad, d_source[None]


def solution(mesh):
    return jax.shard_map(
        on_device,
        mesh=mesh,
        in_specs=(
            P("node", "rel", None),
            P("node", None, None),
            P("rel", None, None),
            P(),
            P("rel", "node", None, None),
            P("rel", "node"),
            P("rel", "node"),
            P("rel", "node"),
            P("rel", "node", None),
        ),
        out_specs=(P("rel", "node", None), P("node", "rel", None)),
        check_vma=False,
    )
```

```python
import functools

import jax
import jax.numpy as jnp
from jax import lax
from jax.experimental import pallas as pl
from jax.experimental.pallas import tpu as pltpu
from jax.sharding import PartitionSpec as P

MESH = pl.DeviceIdType.MESH
ANY = pl.BlockSpec(memory_space=pl.ANY)
VMEM = pl.BlockSpec(memory_space=pltpu.VMEM)
HBM = pl.BlockSpec(memory_space=pltpu.HBM)

SIDE = 4
NODES = 16
ROWS = 64
QUARTER = 128
TILES = 64
EDGE = 128
FEATURE = 512
BLOCKS = 8
CHUNK = 32


def place():
    rel, node = lax.axis_index("rel"), lax.axis_index("node")
    return (
        lax.div(rel, SIDE),
        lax.rem(rel, SIDE),
        lax.div(node, 2),
        lax.rem(node, 2),
        rel,
        node,
    )


def quarter_of(node):
    return lax.rem(lax.div(node, 2), 2) * 2 + lax.rem(node, 2)


def greet(x, y, rel, node):
    barrier = pltpu.get_barrier_semaphore()

    def call(there):
        pl.semaphore_signal(barrier, inc=1, device_id=there, device_id_type=MESH)

    for k in range(1, SIDE):
        call((lax.rem(x + k, SIDE) * SIDE + y, node))
        call((x * SIDE + lax.rem(y + k, SIDE), node))
    for k in range(1, NODES):
        call((rel, lax.rem(node + k, NODES)))
    pl.semaphore_wait(barrier, 2 * (SIDE - 1) + NODES - 1)


def push(src, dst, send, recv, there):
    copy = pltpu.make_async_remote_copy(
        src_ref=src,
        dst_ref=dst,
        send_sem=send,
        recv_sem=recv,
        device_id=there,
        device_id_type=MESH,
    )
    copy.start()
    return copy


def arrival(ref, sem):
    pltpu.make_async_copy(ref, ref, sem).wait()


class RingGather:
    def __init__(self, block, at, peer, send, recv):
        self.block, self.at, self.peer, self.send, self.recv = (
            block,
            at,
            peer,
            send,
            recv,
        )
        self.copies = []

    def move(self, view, number, k):
        self.copies.append(
            push(
                view,
                view,
                self.send.at[number],
                self.recv.at[number],
                self.peer(k),
            )
        )

    def place(self, k):
        return lax.rem(self.at + k, SIDE)

    def begin(self):
        mine = self.block(self.at, None)
        self.move(mine, 0, 1)
        self.move(mine, 1, SIDE - 1)

    def forward(self):
        arrival(self.block(self.place(3), None), self.recv.at[0])
        self.move(self.block(self.place(3), 0), 2, 1)
        arrival(self.block(self.place(1), None), self.recv.at[1])
        self.move(self.block(self.place(1), 1), 3, SIDE - 1)

    def finish(self):
        arrival(self.block(self.place(2), 0), self.recv.at[2])
        arrival(self.block(self.place(2), 1), self.recv.at[3])

    def sent(self):
        for copy in self.copies:
            copy.wait_send()


def gather_kernel(
    adj,
    layer,
    tiles,
    meta,
    t_all,
    a_all,
    x_all,
    m_all,
    local_sem,
    f_send,
    f_recv,
    a_send,
    a_recv,
    x_send,
    x_recv,
    z_send,
    z_recv,
    t_send,
    t_recv,
    s_send,
    s_recv,
    m_send,
    m_recv,
):
    x, y, z, c, rel, node = place()
    half = ROWS // 2
    own = 1 + c
    near = 3 * c
    other = 2 - c
    sibling = (rel, z * 2 + (1 - c))
    beside = lax.rem(z + 7 + 2 * c, 8)
    away = 3 * (1 - c)
    halves = TILES // 2

    def x_peer(k):
        return (lax.rem(x + k, SIDE) * SIDE + y, node)

    def y_peer(k):
        return (x * SIDE + lax.rem(y + k, SIDE), node)

    every = slice(None)
    low, high = pl.ds(0, half), pl.ds(half, half)

    def part_of(h):
        return every if h is None else pl.ds(2 * h, 2)

    def second_leg(slot, number):
        return (
            RingGather(
                lambda p, h: a_all.at[slot, part_of(h), p, low],
                y,
                y_peer,
                a_send.at[number, 0],
                a_recv.at[number, 0],
            ),
            RingGather(
                lambda p, h: a_all.at[slot, p, part_of(h), high],
                x,
                x_peer,
                a_send.at[number, 1],
                a_recv.at[number, 1],
            ),
        )

    a_rings = (second_leg(own, 0), second_leg(near, 1))

    streams = ((2, 4, 2), (6, 4, 2), (10, 3, 2), (13, 3, 1))

    def x_view(stream, px, py, h):
        base, count, cut = streams[stream]
        shards = (pl.ds(base, cut), pl.ds(base + cut, count - cut))
        return x_all.at[pl.ds(base, count) if h is None else shards[h], px, py]

    def x_ring(stream, leg):
        number = 2 * stream + leg
        along_x = (stream + leg) % 2 == 0
        if along_x:
            others = y if leg == 0 else every
            return RingGather(
                lambda p, h: x_view(stream, p, others, h),
                x,
                x_peer,
                x_send.at[number],
                x_recv.at[number],
            )
        others = x if leg == 0 else every
        return RingGather(
            lambda p, h: x_view(stream, others, p, h),
            y,
            y_peer,
            x_send.at[number],
            x_recv.at[number],
        )

    x_rings = [[x_ring(stream, leg) for leg in range(2)] for stream in range(4)]

    greet(x, y, rel, node)

    a_near = push(
        adj,
        a_all.at[away, x, y],
        t_send.at[2],
        t_recv.at[2],
        (rel, beside * 2 + 1 - c),
    )

    a_first = ([], [])

    def a_send_first(source, slot, number):
        for k in range(1, SIDE):
            for rows, peer, stream in ((low, x_peer, 0), (high, y_peer, 1)):
                at = (number, stream, k - 1)
                a_first[number].append(
                    push(
                        source.at[rows],
                        a_all.at[slot, x, y, rows],
                        f_send.at[at],
                        f_recv.at[at],
                        peer(k),
                    )
                )

    a_send_first(adj, own, 0)
    a_own = pltpu.make_async_copy(adj, a_all.at[own, x, y], local_sem.at[0])
    a_own.start()

    def columns(there):
        return pl.ds(pl.multiple_of(quarter_of(there) * QUARTER, QUARTER), QUARTER)

    z_copies = []
    for k in (1, 7, 2, 6, 3, 5, 4):
        for core in range(2):
            there = lax.rem(z + k, 8) * 2 + core
            index = (8 - k) * 2 + c
            z_copies.append(
                push(
                    layer.at[x, y, :, columns(there)],
                    x_all.at[index, x, y],
                    z_send.at[2 * k + core - 2],
                    z_recv.at[index - 2],
                    (rel, there),
                )
            )

    arrival(a_all.at[near, x, y], t_recv.at[2])
    a_send_first(a_all.at[near, x, y], near, 1)

    t_near = push(tiles, t_all.at[own], s_send.at[0], s_recv.at[0], sibling)
    m_copies = [push(meta, m_all.at[own], m_send.at[0], m_recv.at[0], sibling)]
    for h in range(2):
        m_copies.append(
            push(
                meta,
                m_all.at[away],
                m_send.at[1 + h],
                m_recv.at[1 + c],
                (rel, beside * 2 + h),
            )
        )
    m_own = pltpu.make_async_copy(meta, m_all.at[own], local_sem.at[2])
    m_own.start()

    x_near = push(
        layer.at[:, :, :, columns(z * 2 + 1 - c)],
        x_all.at[c],
        s_send.at[4],
        s_recv.at[4],
        sibling,
    )
    x_own = pltpu.make_async_copy(
        layer.at[:, :, :, columns(node)], x_all.at[c], local_sem.at[1]
    )
    x_own.start()

    a_own.wait()
    for number in range(2):
        for copy in a_first[number]:
            copy.wait_recv()
        for ring in a_rings[number]:
            ring.begin()

    for stream in range(4):
        base, count, _ = streams[stream]
        for index in range(base, base + count):
            arrival(x_all.at[index, x, y], z_recv.at[index - 2])
        x_rings[stream][0].begin()
    t_far = []
    for h in range(2):
        part = pl.ds(h * halves, halves)
        t_far.append(
            push(
                tiles.at[part],
                t_all.at[away, part],
                t_send.at[h],
                t_recv.at[c],
                (rel, beside * 2 + h),
            )
        )
    for ring in a_rings[0] + a_rings[1]:
        ring.forward()
    for stream in range(4):
        x_rings[stream][0].forward()
    for stream in range(4):
        x_rings[stream][0].finish()
        x_rings[stream][1].begin()
    for ring in a_rings[0] + a_rings[1]:
        ring.finish()
    pair = pl.ds(2 * c, 2)
    a_over = push(a_all.at[pair], a_all.at[pair], s_send.at[1], s_recv.at[1], sibling)
    for stream in range(4):
        x_rings[stream][1].forward()

    onward = []
    mine = pl.ds(c * halves, halves)
    for sender, slot in ((0, 3), (1, 0)):
        arrival(t_all.at[slot, mine], t_recv.at[sender])
        onward.append(
            push(
                t_all.at[slot, mine],
                t_all.at[slot, mine],
                s_send.at[2 + sender],
                s_recv.at[2 + sender],
                sibling,
            )
        )
    for stream in range(4):
        x_rings[stream][1].finish()

    arrival(t_all.at[other], s_recv.at[0])
    arrival(a_all.at[pl.ds(2 - 2 * c, 2)], s_recv.at[1])
    theirs = pl.ds((1 - c) * halves, halves)
    for sender, slot in ((0, 3), (1, 0)):
        arrival(t_all.at[slot, theirs], s_recv.at[2 + sender])
    arrival(m_all.at[other], m_recv.at[0])
    arrival(m_all.at[3], m_recv.at[1])
    arrival(m_all.at[0], m_recv.at[2])
    m_own.wait()
    x_own.wait()
    arrival(x_all.at[1 - c], s_recv.at[4])
    for ring in a_rings[0] + a_rings[1]:
        ring.sent()
    for rings in x_rings:
        for ring in rings:
            ring.sent()
    for copy in (
        [a_near, t_near, a_over, x_near]
        + a_first[0]
        + a_first[1]
        + z_copies
        + m_copies
        + t_far
        + onward
    ):
        copy.wait_send()


def gather(adj, layer, tiles, meta):
    dma = pltpu.SemaphoreType.DMA
    return pl.pallas_call(
        gather_kernel,
        out_shape=(
            jax.ShapeDtypeStruct((4, TILES, EDGE, EDGE), jnp.bfloat16),
            jax.ShapeDtypeStruct((4, SIDE, SIDE, ROWS, FEATURE), jnp.bfloat16),
            jax.ShapeDtypeStruct((NODES, SIDE, SIDE, ROWS, QUARTER), jnp.bfloat16),
            jax.ShapeDtypeStruct((4, 8, 128), jnp.int32),
        ),
        in_specs=[ANY] * 4,
        out_specs=(ANY,) * 4,
        scratch_shapes=[
            dma((3,)),
            dma((2, 2, 3)),
            dma((2, 2, 3)),
            dma((2, 2, 4)),
            dma((2, 2, 4)),
            dma((8, 4)),
            dma((8, 4)),
            dma((14,)),
            dma((14,)),
            dma((3,)),
            dma((3,)),
            dma((5,)),
            dma((5,)),
            dma((3,)),
            dma((3,)),
        ],
        compiler_params=pltpu.CompilerParams(collective_id=0, has_side_effects=True),
        cost_estimate=pl.CostEstimate(
            flops=0, bytes_accessed=32 << 20, transcendentals=0
        ),
        name="gather_rows_and_tiles",
    )(adj, layer, tiles, meta)


def local_kernel(
    meta_in,
    own_tiles,
    tiles_in,
    a_in,
    x_in,
    weights_in,
    d_out,
    g_out,
    tiles,
    a_rows,
    x_rows,
    weights,
    d_turned,
    aw,
    d_sum,
    h_sum,
    h_turned,
    meta,
    in_sem,
    tile_sem,
    out_sem,
):
    quarter = quarter_of(lax.axis_index("node"))
    shards = 4
    buckets = NODES * BLOCKS
    width = 4 * EDGE
    chunks = shards * TILES // CHUNK
    column = pl.multiple_of(quarter * QUARTER, QUARTER)

    def fetch(src, dst, sem):
        copy = pltpu.make_async_copy(src, dst, sem)
        copy.start()
        return copy

    get_meta = fetch(meta_in, meta, in_sem.at[6])
    get_w = fetch(weights_in.at[:, pl.ds(column, QUARTER)], weights, in_sem.at[0])
    get_a = [
        fetch(
            a_in.at[pl.ds(s * BLOCKS, BLOCKS)],
            a_rows.at[pl.ds(s * BLOCKS, BLOCKS)],
            in_sem.at[1 + s],
        )
        for s in range(shards)
    ]
    get_x = fetch(x_in, x_rows, in_sem.at[5])

    core = lax.rem(lax.axis_index("node"), 2)
    chip = lax.div(lax.axis_index("node"), 2)
    each = TILES // CHUNK

    def tile_copy(n):
        part = pl.ds(n * CHUNK, CHUNK)
        return pltpu.make_async_copy(tiles_in.at[part], tiles.at[part], tile_sem.at[n])

    for i in range(each):
        n = (1 + core) * each + i
        pltpu.make_async_copy(
            own_tiles.at[pl.ds(i * CHUNK, CHUNK)],
            tiles.at[pl.ds(n * CHUNK, CHUNK)],
            tile_sem.at[n],
        ).start()
        tile_copy(i).start()
        tile_copy((2 - core) * each + i).start()
        tile_copy(3 * each + i).start()

    d_sum[...] = jnp.zeros_like(d_sum)
    h_sum[...] = jnp.zeros_like(h_sum)

    get_w.wait()
    both = weights[...].reshape(2 * QUARTER, FEATURE)
    for b in range(shards * BLOCKS // 4):
        if b % 2 == 0:
            get_a[b // 2].wait()
        rows = a_rows[pl.ds(b * 4, 4)].reshape(width, FEATURE)
        value = lax.dot_general(
            both,
            rows,
            (((1,), (1,)), ((), ())),
            preferred_element_type=jnp.float32,
        ).astype(jnp.bfloat16)
        for r in range(2):
            for i in range(4):
                aw[r, b * 4 + i] = value[
                    r * QUARTER : (r + 1) * QUARTER, i * EDGE : (i + 1) * EDGE
                ]
    get_x.wait()
    get_meta.wait()

    def some(n, carry):
        tile_copy(n).wait()
        slot = lax.div(n * CHUNK, TILES)
        first = lax.rem(n * CHUNK, TILES)
        for k in range(CHUNK):
            code = meta[slot, 0, first + k]
            target = slot * BLOCKS + lax.rem(code, BLOCKS)
            relation = lax.rem(lax.div(code, BLOCKS), 2)
            bucket = lax.div(code, 2 * BLOCKS)
            tile = tiles[n * CHUNK + k]
            d_sum[bucket] += jnp.dot(
                aw[relation, target], tile, preferred_element_type=jnp.float32
            )
            h_sum[relation, target] += jnp.dot(
                tile, x_rows[jnp.bitwise_and(bucket - 16 * chip, 127)],
                preferred_element_type=jnp.float32
            )
        return carry

    lax.fori_loop(0, chunks, some, 0)

    def out_copy(n):
        part = pl.ds(n * 16, 16)
        return pltpu.make_async_copy(d_turned.at[part], d_out.at[part], out_sem.at[n])

    def turn(n, carry):
        for k in range(16):
            d_turned[n * 16 + k] = d_sum[n * 16 + k].astype(jnp.bfloat16).T
        out_copy(n).start()
        return carry

    lax.fori_loop(0, buckets // 16, turn, 0)
    for r in range(2):
        for b in range(shards * BLOCKS):
            h_turned[:, pl.ds(b * EDGE, EDGE)] = h_sum[r, b].astype(jnp.bfloat16).T
        g_out[r] = jnp.dot(
            h_turned[...],
            a_rows[...].reshape(shards * BLOCKS * EDGE, FEATURE),
            preferred_element_type=jnp.float32,
        )
    for n in range(buckets // 16):
        out_copy(n).wait()


def local(meta, own_tiles, tiles, a_rows, x_rows, weights):
    buckets = NODES * BLOCKS
    shards = 4
    bf16 = jnp.bfloat16
    return pl.pallas_call(
        local_kernel,
        out_shape=(
            jax.ShapeDtypeStruct((buckets, EDGE, QUARTER), bf16),
            jax.ShapeDtypeStruct((2, QUARTER, FEATURE), jnp.float32),
        ),
        in_specs=[HBM, ANY, HBM, HBM, HBM, HBM],
        out_specs=(ANY, VMEM),
        scratch_shapes=[
            pltpu.VMEM((shards * TILES, EDGE, EDGE), bf16),
            pltpu.VMEM((shards * BLOCKS, EDGE, FEATURE), bf16),
            pltpu.VMEM((buckets, EDGE, QUARTER), bf16),
            pltpu.VMEM((2, QUARTER, FEATURE), bf16),
            pltpu.VMEM((buckets, EDGE, QUARTER), bf16),
            pltpu.VMEM((2, shards * BLOCKS, QUARTER, EDGE), bf16),
            pltpu.VMEM((buckets, QUARTER, EDGE), jnp.float32),
            pltpu.VMEM((2, shards * BLOCKS, EDGE, QUARTER), jnp.float32),
            pltpu.VMEM((QUARTER, shards * BLOCKS * EDGE), bf16),
            pltpu.SMEM((shards, 8, 128), jnp.int32),
            pltpu.SemaphoreType.DMA((7,)),
            pltpu.SemaphoreType.DMA((shards * TILES // CHUNK,)),
            pltpu.SemaphoreType.DMA((buckets // 16,)),
        ],
        compiler_params=pltpu.CompilerParams(vmem_limit_bytes=40 << 20),
        name="tile_products",
    )(meta, own_tiles, tiles, a_rows, x_rows, weights)


class RingSum:
    def __init__(self, term, send_term, at, peer, got, out, send, recv):
        self.term, self.send_term, self.at, self.peer = term, send_term, at, peer
        self.got, self.out, self.send, self.recv = got, out, send, recv
        self.copies = []

    def place(self, k):
        return lax.rem(self.at + k, SIDE)

    def move(self, view, number, k):
        self.copies.append(
            push(
                view,
                self.got.at[number],
                self.send.at[number],
                self.recv.at[number],
                self.peer(k),
            )
        )

    def begin(self):
        self.move(self.send_term(self.place(2), 0), 0, SIDE - 1)
        self.move(self.send_term(self.place(2), 1), 1, 1)

    def direct(self):
        self.move(self.send_term(self.place(1), 0), 2, 1)
        self.move(self.send_term(self.place(3), 1), 3, SIDE - 1)

    def pass_on(self):
        for number, k, h in ((0, SIDE - 1, 0), (1, 1, 1)):
            arrival(self.got.at[number], self.recv.at[number])
            value = f32(self.term(self.place(k), h)[...]) + f32(self.got[number])
            self.out[h] = value.astype(jnp.bfloat16)
            self.move(self.out.at[h], 4 + h, k)

    def result(self, h):
        for number in (2 + h, 4 + h):
            arrival(self.got.at[number], self.recv.at[number])
        value = f32(self.got[2 + h]) + f32(self.got[4 + h])
        return (value + f32(self.term(self.at, h)[...])).astype(jnp.bfloat16)

    def sent(self):
        for copy in self.copies:
            copy.wait_send()


def f32(value):
    return value.astype(jnp.float32)


def reduce_kernel(
    d_part,
    g_part,
    adj_in,
    self_weight_in,
    g_out,
    d_out,
    d_here,
    got_first,
    out_first,
    got_second,
    out_second,
    summed,
    total,
    got_z,
    got_g,
    adj,
    self_weight,
    local_sem,
    d_sem,
    r_send,
    r_recv,
    z_send,
    z_recv,
    g_send,
    g_recv,
):
    x, y, z, c, rel, node = place()
    quarter = quarter_of(node)
    streams = 4

    def x_peer(k):
        return (lax.rem(x + k, SIDE) * SIDE + y, node)

    def y_peer(k):
        return (x * SIDE + lax.rem(y + k, SIDE), node)

    def fetch(src, dst, sem):
        copy = pltpu.make_async_copy(src, dst, sem)
        copy.start()
        return copy

    get_d = []
    for stream in range(streams):
        part = pl.ds(4 * stream, 4)
        get_d.append(fetch(d_part.at[part], d_here.at[part], d_sem.at[stream]))
    get_adj = fetch(adj_in, adj, local_sem.at[0])
    get_weight = fetch(self_weight_in, self_weight, local_sem.at[1])

    def first_ring(stream):
        along_x = stream % 2 == 0

        def view(ref, p, h):
            shards = pl.ds(4 * stream + 2 * h, 2)
            return ref.at[shards, p] if along_x else ref.at[shards, :, p]

        return RingSum(
            lambda p, h: view(d_here, p, h),
            lambda p, h: view(d_part, p, h),
            x if along_x else y,
            x_peer if along_x else y_peer,
            got_first.at[stream],
            out_first.at[stream],
            r_send.at[2 * stream],
            r_recv.at[2 * stream],
        )

    def second_ring(stream):
        along_x = stream % 2 == 1

        def view(p, h):
            return summed.at[stream, pl.ds(2 * h, 2), p]

        return RingSum(
            view,
            view,
            x if along_x else y,
            x_peer if along_x else y_peer,
            got_second.at[stream],
            out_second.at[stream],
            r_send.at[2 * stream + 1],
            r_recv.at[2 * stream + 1],
        )

    firsts = [first_ring(stream) for stream in range(streams)]
    seconds = [second_ring(stream) for stream in range(streams)]

    greet(x, y, rel, node)

    for ring in firsts:
        ring.begin()
    for ring in firsts[:2]:
        ring.direct()

    sender = lax.div(z, 2)
    for m in range(4):
        owner = quarter * 4 + m
        rows = g_part.at[:, pl.ds(32 * m, 32), :]

        @pl.when(owner != node)
        def _():
            push(
                rows,
                got_g.at[sender],
                g_send.at[m],
                g_recv.at[sender],
                (rel, owner),
            )

        @pl.when(owner == node)
        def _():
            pltpu.make_async_copy(rows, got_g.at[sender], g_recv.at[sender]).start()

    def middle(stream):
        for h in range(2):
            summed[stream, pl.ds(2 * h, 2)] = firsts[stream].result(h)
        seconds[stream].begin()
        seconds[stream].direct()

    def last(stream):
        for h in range(2):
            total[pl.ds(4 * stream + 2 * h, 2)] = seconds[stream].result(h)
        for n in range(4 * stream, 4 * stream + 4):

            @pl.when(node != n)
            def _():
                push(
                    total.at[n],
                    got_z.at[node],
                    z_send.at[n],
                    z_recv.at[node],
                    (rel, n),
                )

            @pl.when(node == n)
            def _():
                pltpu.make_async_copy(
                    total.at[n], got_z.at[node], z_recv.at[node]
                ).start()

    for stream in range(streams):
        get_d[stream].wait()
    for ring in firsts[:2]:
        ring.pass_on()
    for ring in firsts[2:]:
        ring.direct()
    for ring in firsts[2:]:
        ring.pass_on()
    middle(0)
    middle(1)
    seconds[0].pass_on()
    seconds[1].pass_on()
    middle(2)
    middle(3)
    last(0)
    last(1)
    seconds[2].pass_on()
    seconds[3].pass_on()
    last(2)
    last(3)

    get_adj.wait()
    get_weight.wait()
    own_term = lax.dot_general(
        adj[...],
        self_weight[...],
        (((1,), (1,)), ((), ())),
        preferred_element_type=jnp.float32,
    )

    for m in range(4):
        arrival(got_g.at[m], g_recv.at[m])
    g_out[...] = (got_g[0] + got_g[1]) + (got_g[2] + got_g[3])

    for n in range(NODES):
        arrival(got_z.at[n], z_recv.at[n])
    for q in range(4):
        value = own_term[:, q * QUARTER : (q + 1) * QUARTER]
        for step in range(4):
            value = value + f32(got_z[(2 * step + q // 2) * 2 + q % 2])
        d_out[:, q * QUARTER : (q + 1) * QUARTER] = value.astype(jnp.bfloat16)

    for ring in firsts + seconds:
        ring.sent()
    for m in range(4):
        owner = quarter * 4 + m

        @pl.when(owner != node)
        def _():
            pltpu.make_async_remote_copy(
                src_ref=g_part.at[:, pl.ds(32 * m, 32), :],
                dst_ref=got_g.at[sender],
                send_sem=g_send.at[m],
                recv_sem=g_recv.at[sender],
                device_id=(rel, owner),
                device_id_type=MESH,
            ).wait_send()

    for n in range(NODES):

        @pl.when(node != n)
        def _():
            pltpu.make_async_remote_copy(
                src_ref=total.at[n],
                dst_ref=got_z.at[node],
                send_sem=z_send.at[n],
                recv_sem=z_recv.at[node],
                device_id=(rel, n),
                device_id_type=MESH,
            ).wait_send()


def reduce(d_part, g_part, adj, self_weight):
    dma = pltpu.SemaphoreType.DMA
    bf16 = jnp.bfloat16
    return pl.pallas_call(
        reduce_kernel,
        out_shape=(
            jax.ShapeDtypeStruct((2, 32, FEATURE), jnp.float32),
            jax.ShapeDtypeStruct((ROWS, FEATURE), bf16),
        ),
        in_specs=[ANY, ANY, ANY, ANY],
        out_specs=(VMEM, VMEM),
        scratch_shapes=[
            pltpu.VMEM((NODES, SIDE, SIDE, ROWS, QUARTER), bf16),
            pltpu.VMEM((4, 6, 2, SIDE, ROWS, QUARTER), bf16),
            pltpu.VMEM((4, 2, 2, SIDE, ROWS, QUARTER), bf16),
            pltpu.VMEM((4, 6, 2, ROWS, QUARTER), bf16),
            pltpu.VMEM((4, 2, 2, ROWS, QUARTER), bf16),
            pltpu.VMEM((4, 4, SIDE, ROWS, QUARTER), bf16),
            pltpu.VMEM((NODES, ROWS, QUARTER), bf16),
            pltpu.VMEM((NODES, ROWS, QUARTER), bf16),
            pltpu.VMEM((4, 2, 32, FEATURE), jnp.float32),
            pltpu.VMEM((ROWS, FEATURE), bf16),
            pltpu.VMEM((FEATURE, FEATURE), bf16),
            dma((2,)),
            dma((4,)),
            dma((8, 6)),
            dma((8, 6)),
            dma((16,)),
            dma((16,)),
            dma((4,)),
            dma((4,)),
        ],
        compiler_params=pltpu.CompilerParams(
            collective_id=1, has_side_effects=True, vmem_limit_bytes=24 << 20
        ),
        name="sum_terms",
    )(d_part, g_part, adj, self_weight)


def on_device(
    out_adjoint,
    layer_input,
    rel_weights,
    self_weight,
    tile_values,
    tile_rel,
    tile_target,
    tile_src,
    tile_dest,
):
    code = (
        (tile_dest[:, :, 0] * BLOCKS + tile_src) * 2 + tile_rel
    ) * BLOCKS + tile_target
    meta = jnp.pad(code, ((0, 7), (0, 128 - TILES)))
    adj = out_adjoint[0]
    tiles, a_rows, x_rows, codes = gather(
        adj,
        layer_input.reshape(SIDE, SIDE, ROWS, FEATURE),
        tile_values[0],
        meta,
    )
    stay = functools.partial(
        pltpu.with_memory_space_constraint, memory_space=pltpu.HBM
    )
    d_part, g_part = local(
        stay(codes),
        tile_values[0],
        stay(tiles.reshape(4 * TILES, EDGE, EDGE)),
        stay(a_rows.reshape(4 * BLOCKS, EDGE, FEATURE)),
        stay(x_rows.reshape(NODES * BLOCKS, EDGE, QUARTER)),
        stay(rel_weights),
    )
    rel_weight_grad, d_source = reduce(
        d_part.reshape(NODES, SIDE, SIDE, ROWS, QUARTER), g_part, adj, self_weight
    )
    return rel_weight_grad, d_source[None]


def solution(mesh):
    return jax.shard_map(
        on_device,
        mesh=mesh,
        in_specs=(
            P("node", "rel", None),
            P("node", None, None),
            P("rel", None, None),
            P(),
            P("rel", "node", None, None),
            P("rel", "node"),
            P("rel", "node"),
            P("rel", "node"),
            P("rel", "node", None),
        ),
        out_specs=(P("rel", "node", None), P("node", "rel", None)),
        check_vma=False,
    )
```

```python
import functools

import jax
import jax.numpy as jnp
from jax import lax
from jax.experimental import pallas as pl
from jax.experimental.pallas import tpu as pltpu
from jax.sharding import PartitionSpec as P

MESH = pl.DeviceIdType.MESH
ANY = pl.BlockSpec(memory_space=pl.ANY)
VMEM = pl.BlockSpec(memory_space=pltpu.VMEM)
HBM = pl.BlockSpec(memory_space=pltpu.HBM)

SIDE = 4
NODES = 16
ROWS = 64
QUARTER = 128
TILES = 64
EDGE = 128
FEATURE = 512
BLOCKS = 8
CHUNK = 32


def place():
    rel, node = lax.axis_index("rel"), lax.axis_index("node")
    return (
        lax.div(rel, SIDE),
        lax.rem(rel, SIDE),
        lax.div(node, 2),
        lax.rem(node, 2),
        rel,
        node,
    )


def quarter_of(node):
    return lax.rem(lax.div(node, 2), 2) * 2 + lax.rem(node, 2)


def greet(x, y, rel, node):
    barrier = pltpu.get_barrier_semaphore()

    def call(there):
        pl.semaphore_signal(barrier, inc=1, device_id=there, device_id_type=MESH)

    for k in range(1, SIDE):
        call((lax.rem(x + k, SIDE) * SIDE + y, node))
        call((x * SIDE + lax.rem(y + k, SIDE), node))
    for k in range(1, NODES):
        call((rel, lax.rem(node + k, NODES)))
    pl.semaphore_wait(barrier, 2 * (SIDE - 1) + NODES - 1)


def push(src, dst, send, recv, there):
    copy = pltpu.make_async_remote_copy(
        src_ref=src,
        dst_ref=dst,
        send_sem=send,
        recv_sem=recv,
        device_id=there,
        device_id_type=MESH,
    )
    copy.start()
    return copy


def arrival(ref, sem):
    pltpu.make_async_copy(ref, ref, sem).wait()


class RingGather:
    def __init__(self, block, at, peer, send, recv):
        self.block, self.at, self.peer, self.send, self.recv = (
            block,
            at,
            peer,
            send,
            recv,
        )
        self.copies = []

    def move(self, view, number, k):
        self.copies.append(
            push(
                view,
                view,
                self.send.at[number],
                self.recv.at[number],
                self.peer(k),
            )
        )

    def place(self, k):
        return lax.rem(self.at + k, SIDE)

    def begin(self):
        mine = self.block(self.at, None)
        self.move(mine, 0, 1)
        self.move(mine, 1, SIDE - 1)

    def forward(self):
        arrival(self.block(self.place(3), None), self.recv.at[0])
        self.move(self.block(self.place(3), 0), 2, 1)
        arrival(self.block(self.place(1), None), self.recv.at[1])
        self.move(self.block(self.place(1), 1), 3, SIDE - 1)

    def finish(self):
        arrival(self.block(self.place(2), 0), self.recv.at[2])
        arrival(self.block(self.place(2), 1), self.recv.at[3])

    def sent(self):
        for copy in self.copies:
            copy.wait_send()


def gather_kernel(
    adj,
    layer,
    tiles,
    meta,
    t_all,
    a_all,
    x_all,
    m_all,
    local_sem,
    f_send,
    f_recv,
    a_send,
    a_recv,
    x_send,
    x_recv,
    z_send,
    z_recv,
    t_send,
    t_recv,
    s_send,
    s_recv,
    m_send,
    m_recv,
):
    x, y, z, c, rel, node = place()
    half = ROWS // 2
    own = 1 + c
    near = 3 * c
    other = 2 - c
    sibling = (rel, z * 2 + (1 - c))
    beside = lax.rem(z + 7 + 2 * c, 8)
    away = 3 * (1 - c)
    halves = TILES // 2

    def x_peer(k):
        return (lax.rem(x + k, SIDE) * SIDE + y, node)

    def y_peer(k):
        return (x * SIDE + lax.rem(y + k, SIDE), node)

    every = slice(None)
    low, high = pl.ds(0, half), pl.ds(half, half)

    def part_of(h):
        return every if h is None else pl.ds(2 * h, 2)

    def second_leg(slot, number):
        return (
            RingGather(
                lambda p, h: a_all.at[slot, part_of(h), p, low],
                y,
                y_peer,
                a_send.at[number, 0],
                a_recv.at[number, 0],
            ),
            RingGather(
                lambda p, h: a_all.at[slot, p, part_of(h), high],
                x,
                x_peer,
                a_send.at[number, 1],
                a_recv.at[number, 1],
            ),
        )

    a_rings = (second_leg(own, 0), second_leg(near, 1))

    streams = ((2, 4, 2), (6, 4, 2), (10, 3, 2), (13, 3, 1))

    def x_view(stream, px, py, h):
        base, count, cut = streams[stream]
        shards = (pl.ds(base, cut), pl.ds(base + cut, count - cut))
        return x_all.at[pl.ds(base, count) if h is None else shards[h], px, py]

    def x_ring(stream, leg):
        number = 2 * stream + leg
        along_x = (stream + leg) % 2 == 0
        if along_x:
            others = y if leg == 0 else every
            return RingGather(
                lambda p, h: x_view(stream, p, others, h),
                x,
                x_peer,
                x_send.at[number],
                x_recv.at[number],
            )
        others = x if leg == 0 else every
        return RingGather(
            lambda p, h: x_view(stream, others, p, h),
            y,
            y_peer,
            x_send.at[number],
            x_recv.at[number],
        )

    x_rings = [[x_ring(stream, leg) for leg in range(2)] for stream in range(4)]

    greet(x, y, rel, node)

    a_near = push(
        adj,
        a_all.at[away, x, y],
        t_send.at[2],
        t_recv.at[2],
        (rel, beside * 2 + 1 - c),
    )

    a_first = ([], [])

    def a_send_first(source, slot, number):
        for k in range(1, SIDE):
            for rows, peer, stream in ((low, x_peer, 0), (high, y_peer, 1)):
                at = (number, stream, k - 1)
                a_first[number].append(
                    push(
                        source.at[rows],
                        a_all.at[slot, x, y, rows],
                        f_send.at[at],
                        f_recv.at[at],
                        peer(k),
                    )
                )

    a_send_first(adj, own, 0)
    a_own = pltpu.make_async_copy(adj, a_all.at[own, x, y], local_sem.at[0])
    a_own.start()

    def columns(there):
        return pl.ds(pl.multiple_of(quarter_of(there) * QUARTER, QUARTER), QUARTER)

    z_copies = []
    for k in (1, 7, 2, 6, 3, 5, 4):
        for core in range(2):
            there = lax.rem(z + k, 8) * 2 + core
            index = (8 - k) * 2 + c
            z_copies.append(
                push(
                    layer.at[x, y, :, columns(there)],
                    x_all.at[index, x, y],
                    z_send.at[2 * k + core - 2],
                    z_recv.at[index - 2],
                    (rel, there),
                )
            )

    arrival(a_all.at[near, x, y], t_recv.at[2])
    a_send_first(a_all.at[near, x, y], near, 1)

    t_near = push(tiles, t_all.at[own], s_send.at[0], s_recv.at[0], sibling)
    m_copies = [push(meta, m_all.at[own], m_send.at[0], m_recv.at[0], sibling)]
    for h in range(2):
        m_copies.append(
            push(
                meta,
                m_all.at[away],
                m_send.at[1 + h],
                m_recv.at[1 + c],
                (rel, beside * 2 + h),
            )
        )
    m_own = pltpu.make_async_copy(meta, m_all.at[own], local_sem.at[2])
    m_own.start()

    x_near = push(
        layer.at[:, :, :, columns(z * 2 + 1 - c)],
        x_all.at[c],
        s_send.at[4],
        s_recv.at[4],
        sibling,
    )
    x_own = pltpu.make_async_copy(
        layer.at[:, :, :, columns(node)], x_all.at[c], local_sem.at[1]
    )
    x_own.start()

    a_own.wait()
    for number in range(2):
        for copy in a_first[number]:
            copy.wait_recv()
        for ring in a_rings[number]:
            ring.begin()

    for stream in range(4):
        base, count, _ = streams[stream]
        for index in range(base, base + count):
            arrival(x_all.at[index, x, y], z_recv.at[index - 2])
        x_rings[stream][0].begin()
    t_far = []
    for h in range(2):
        part = pl.ds(h * halves, halves)
        t_far.append(
            push(
                tiles.at[part],
                t_all.at[away, part],
                t_send.at[h],
                t_recv.at[c],
                (rel, beside * 2 + h),
            )
        )
    for ring in a_rings[0] + a_rings[1]:
        ring.forward()
    for stream in range(4):
        x_rings[stream][0].forward()
    for stream in range(4):
        x_rings[stream][0].finish()
        x_rings[stream][1].begin()
    for ring in a_rings[0] + a_rings[1]:
        ring.finish()
    pair = pl.ds(2 * c, 2)
    a_over = push(a_all.at[pair], a_all.at[pair], s_send.at[1], s_recv.at[1], sibling)
    for stream in range(4):
        x_rings[stream][1].forward()

    onward = []
    mine = pl.ds(c * halves, halves)
    for sender, slot in ((0, 3), (1, 0)):
        arrival(t_all.at[slot, mine], t_recv.at[sender])
        onward.append(
            push(
                t_all.at[slot, mine],
                t_all.at[slot, mine],
                s_send.at[2 + sender],
                s_recv.at[2 + sender],
                sibling,
            )
        )
    for stream in range(4):
        x_rings[stream][1].finish()

    arrival(t_all.at[other], s_recv.at[0])
    arrival(a_all.at[pl.ds(2 - 2 * c, 2)], s_recv.at[1])
    theirs = pl.ds((1 - c) * halves, halves)
    for sender, slot in ((0, 3), (1, 0)):
        arrival(t_all.at[slot, theirs], s_recv.at[2 + sender])
    arrival(m_all.at[other], m_recv.at[0])
    arrival(m_all.at[3], m_recv.at[1])
    arrival(m_all.at[0], m_recv.at[2])
    m_own.wait()
    x_own.wait()
    arrival(x_all.at[1 - c], s_recv.at[4])
    for ring in a_rings[0] + a_rings[1]:
        ring.sent()
    for rings in x_rings:
        for ring in rings:
            ring.sent()
    for copy in (
        [a_near, t_near, a_over, x_near]
        + a_first[0]
        + a_first[1]
        + z_copies
        + m_copies
        + t_far
        + onward
    ):
        copy.wait_send()


def gather(adj, layer, tiles, meta):
    dma = pltpu.SemaphoreType.DMA
    return pl.pallas_call(
        gather_kernel,
        out_shape=(
            jax.ShapeDtypeStruct((4, TILES, EDGE, EDGE), jnp.bfloat16),
            jax.ShapeDtypeStruct((4, SIDE, SIDE, ROWS, FEATURE), jnp.bfloat16),
            jax.ShapeDtypeStruct((NODES, SIDE, SIDE, ROWS, QUARTER), jnp.bfloat16),
            jax.ShapeDtypeStruct((4, 8, 128), jnp.int32),
        ),
        in_specs=[ANY] * 4,
        out_specs=(VMEM, VMEM, VMEM, ANY),
        scratch_shapes=[
            dma((3,)),
            dma((2, 2, 3)),
            dma((2, 2, 3)),
            dma((2, 2, 4)),
            dma((2, 2, 4)),
            dma((8, 4)),
            dma((8, 4)),
            dma((14,)),
            dma((14,)),
            dma((3,)),
            dma((3,)),
            dma((5,)),
            dma((5,)),
            dma((3,)),
            dma((3,)),
        ],
        compiler_params=pltpu.CompilerParams(
            collective_id=0, has_side_effects=True, vmem_limit_bytes=24 << 20
        ),
        cost_estimate=pl.CostEstimate(
            flops=0, bytes_accessed=32 << 20, transcendentals=0
        ),
        name="gather_rows_and_tiles",
    )(adj, layer, tiles, meta)


def local_kernel(
    meta_in,
    own_tiles,
    tiles,
    a_rows,
    x_rows,
    weights_in,
    d_out,
    g_out,
    weights,
    aw,
    d_sum,
    h_sum,
    h_turned,
    meta,
    in_sem,
):
    quarter = quarter_of(lax.axis_index("node"))
    shards = 4
    buckets = NODES * BLOCKS
    width = 4 * EDGE
    column = pl.multiple_of(quarter * QUARTER, QUARTER)

    def fetch(src, dst, sem):
        copy = pltpu.make_async_copy(src, dst, sem)
        copy.start()
        return copy

    get_meta = fetch(meta_in, meta, in_sem.at[0])
    get_w = fetch(weights_in.at[:, pl.ds(column, QUARTER)], weights, in_sem.at[1])
    core = lax.rem(lax.axis_index("node"), 2)
    chip = lax.div(lax.axis_index("node"), 2)
    each = TILES // CHUNK

    d_sum[...] = jnp.zeros_like(d_sum)
    h_sum[...] = jnp.zeros_like(h_sum)

    get_w.wait()
    both = weights[...].reshape(2 * QUARTER, FEATURE)
    for b in range(shards * BLOCKS // 4):
        rows = a_rows[pl.ds(b * 4, 4)].reshape(width, FEATURE)
        value = lax.dot_general(
            both,
            rows,
            (((1,), (1,)), ((), ())),
            preferred_element_type=jnp.float32,
        ).astype(jnp.bfloat16)
        for r in range(2):
            for i in range(4):
                aw[r, b * 4 + i] = value[
                    r * QUARTER : (r + 1) * QUARTER, i * EDGE : (i + 1) * EDGE
                ]
    get_meta.wait()

    def some(n, source, start):
        slot = lax.div(n * CHUNK, TILES)
        first = lax.rem(n * CHUNK, TILES)
        for k in range(CHUNK):
            code = meta[slot, 0, first + k]
            target = slot * BLOCKS + lax.rem(code, BLOCKS)
            relation = lax.rem(lax.div(code, BLOCKS), 2)
            bucket = jnp.bitwise_and(
                lax.div(code, 2 * BLOCKS) - 16 * chip, buckets - 1
            )
            tile = source[start + k]
            d_sum[bucket] += jnp.dot(
                aw[relation, target], tile, preferred_element_type=jnp.float32
            )
            h_sum[relation, target] += jnp.dot(
                tile, x_rows[bucket], preferred_element_type=jnp.float32
            )

    def own_some(i, carry):
        some((1 + core) * each + i, own_tiles, i * CHUNK)
        return carry

    def other_some(i, carry):
        number = lax.div(i, each)
        slot = lax.rem(4 - core * lax.rem(number, 2) + 2 * lax.rem(number, 2), 4)
        slot = jnp.where(number == 2, 3, slot)
        n = slot * each + lax.rem(i, each)
        some(n, tiles, n * CHUNK)
        return carry

    lax.fori_loop(0, each, own_some, 0)
    lax.fori_loop(0, 3 * each, other_some, 0)

    def turn(n, carry):
        for k in range(16):
            d_out[n * 16 + k] = d_sum[n * 16 + k].astype(jnp.bfloat16).T
        return carry

    lax.fori_loop(0, buckets // 16, turn, 0)
    for r in range(2):
        for b in range(shards * BLOCKS):
            h_turned[:, pl.ds(b * EDGE, EDGE)] = h_sum[r, b].astype(jnp.bfloat16).T
        g_out[r] = jnp.dot(
            h_turned[...],
            a_rows[...].reshape(shards * BLOCKS * EDGE, FEATURE),
            preferred_element_type=jnp.float32,
        )


def local(meta, own_tiles, tiles, a_rows, x_rows, weights):
    buckets = NODES * BLOCKS
    shards = 4
    bf16 = jnp.bfloat16
    return pl.pallas_call(
        local_kernel,
        out_shape=(
            jax.ShapeDtypeStruct((buckets, EDGE, QUARTER), bf16),
            jax.ShapeDtypeStruct((2, QUARTER, FEATURE), jnp.float32),
        ),
        in_specs=[HBM, VMEM, VMEM, VMEM, VMEM, HBM],
        out_specs=(VMEM, VMEM),
        scratch_shapes=[
            pltpu.VMEM((2, QUARTER, FEATURE), bf16),
            pltpu.VMEM((2, shards * BLOCKS, QUARTER, EDGE), bf16),
            pltpu.VMEM((buckets, QUARTER, EDGE), jnp.float32),
            pltpu.VMEM((2, shards * BLOCKS, EDGE, QUARTER), jnp.float32),
            pltpu.VMEM((QUARTER, shards * BLOCKS * EDGE), bf16),
            pltpu.SMEM((shards, 8, 128), jnp.int32),
            pltpu.SemaphoreType.DMA((2,)),
        ],
        compiler_params=pltpu.CompilerParams(vmem_limit_bytes=24 << 20),
        name="tile_products",
    )(meta, own_tiles, tiles, a_rows, x_rows, weights)


class RingSum:
    def __init__(self, term, send_term, at, peer, got, out, send, recv):
        self.term, self.send_term, self.at, self.peer = term, send_term, at, peer
        self.got, self.out, self.send, self.recv = got, out, send, recv
        self.copies = []

    def place(self, k):
        return lax.rem(self.at + k, SIDE)

    def move(self, view, number, k):
        self.copies.append(
            push(
                view,
                self.got.at[number],
                self.send.at[number],
                self.recv.at[number],
                self.peer(k),
            )
        )

    def begin(self):
        self.move(self.send_term(self.place(2), 0), 0, SIDE - 1)
        self.move(self.send_term(self.place(2), 1), 1, 1)

    def direct(self):
        self.move(self.send_term(self.place(1), 0), 2, 1)
        self.move(self.send_term(self.place(3), 1), 3, SIDE - 1)

    def pass_on(self):
        for number, k, h in ((0, SIDE - 1, 0), (1, 1, 1)):
            arrival(self.got.at[number], self.recv.at[number])
            value = f32(self.term(self.place(k), h)[...]) + f32(self.got[number])
            self.out[h] = value.astype(jnp.bfloat16)
            self.move(self.out.at[h], 4 + h, k)

    def result(self, h):
        for number in (2 + h, 4 + h):
            arrival(self.got.at[number], self.recv.at[number])
        value = f32(self.got[2 + h]) + f32(self.got[4 + h])
        return (value + f32(self.term(self.at, h)[...])).astype(jnp.bfloat16)

    def sent(self):
        for copy in self.copies:
            copy.wait_send()


def f32(value):
    return value.astype(jnp.float32)


def reduce_kernel(
    d_part,
    g_part,
    adj_in,
    self_weight_in,
    g_out,
    d_out,
    got_first,
    out_first,
    got_second,
    summed,
    total,
    got_z,
    got_g,
    adj,
    self_weight,
    local_sem,
    r_send,
    r_recv,
    q_send,
    q_recv,
    z_send,
    z_recv,
    g_send,
    g_recv,
):
    x, y, z, c, rel, node = place()
    quarter = quarter_of(node)
    streams = 4

    def x_peer(k):
        return (lax.rem(x + k, SIDE) * SIDE + y, node)

    def y_peer(k):
        return (x * SIDE + lax.rem(y + k, SIDE), node)

    def fetch(src, dst, sem):
        copy = pltpu.make_async_copy(src, dst, sem)
        copy.start()
        return copy

    get_adj = fetch(adj_in, adj, local_sem.at[0])
    get_weight = fetch(self_weight_in, self_weight, local_sem.at[1])

    def first_ring(stream):
        along_x = stream % 2 == 0

        def view(ref, p, h):
            shards = pl.ds(4 * stream + 2 * h, 2)
            return ref.at[shards, p] if along_x else ref.at[shards, :, p]

        return RingSum(
            lambda p, h: view(d_part, p, h),
            lambda p, h: view(d_part, p, h),
            x if along_x else y,
            x_peer if along_x else y_peer,
            got_first.at[stream],
            out_first.at[stream],
            r_send.at[stream],
            r_recv.at[stream],
        )

    firsts = [first_ring(stream) for stream in range(streams)]

    greet(x, y, rel, node)

    for ring in firsts:
        ring.begin()
    for ring in firsts:
        ring.direct()

    sender = lax.div(z, 2)
    for m in range(4):
        owner = quarter * 4 + m
        rows = g_part.at[:, pl.ds(32 * m, 32), :]

        @pl.when(owner != node)
        def _():
            push(
                rows,
                got_g.at[sender],
                g_send.at[m],
                g_recv.at[sender],
                (rel, owner),
            )

        @pl.when(owner == node)
        def _():
            pltpu.make_async_copy(rows, got_g.at[sender], g_recv.at[sender]).start()

    later = []

    def middle(stream):
        for h in range(2):
            summed[stream, pl.ds(2 * h, 2)] = firsts[stream].result(h)
        at, peer = (y, y_peer) if stream % 2 == 0 else (x, x_peer)
        for k in (2, 1, 3):
            later.append(
                push(
                    summed.at[stream, :, lax.rem(at + k, SIDE)],
                    got_second.at[stream, k - 1],
                    q_send.at[stream, k - 1],
                    q_recv.at[stream, k - 1],
                    peer(k),
                )
            )

    z_copies = []

    def last(stream):
        for k in range(SIDE - 1):
            arrival(got_second.at[stream, k], q_recv.at[stream, k])
        value = f32(summed[stream, :, y if stream % 2 == 0 else x])
        for k in range(SIDE - 1):
            value = value + f32(got_second[stream, k])
        total[pl.ds(4 * stream, 4)] = value.astype(jnp.bfloat16)
        for up in (2 * stream, 2 * stream + 1):
            cores = (1 - c,) if up == 0 else (0, 1)
            for number, core in enumerate(cores):
                z_copies.append(
                    push(
                        total.at[2 * up + core],
                        got_z.at[node],
                        z_send.at[2 * up + number],
                        z_recv.at[2 * up + c],
                        (rel, lax.rem(z + up, 8) * 2 + core),
                    )
                )
        if stream == 0:
            got_z[node] = total[c]

    for ring in firsts:
        ring.pass_on()
    middle(0)
    middle(1)
    middle(2)
    middle(3)
    last(0)
    last(1)
    last(2)
    last(3)

    get_adj.wait()
    get_weight.wait()
    own_term = lax.dot_general(
        adj[...],
        self_weight[...],
        (((1,), (1,)), ((), ())),
        preferred_element_type=jnp.float32,
    )

    for m in range(4):
        arrival(got_g.at[m], g_recv.at[m])
    g_out[...] = (got_g[0] + got_g[1]) + (got_g[2] + got_g[3])

    arrival(got_z.at[z * 2 + 1 - c], z_recv.at[1 - c])
    for up in range(1, 8):
        for core in range(2):
            arrival(
                got_z.at[lax.rem(z + 8 - up, 8) * 2 + core], z_recv.at[2 * up + core]
            )
    for q in range(4):
        value = own_term[:, q * QUARTER : (q + 1) * QUARTER]
        for step in range(4):
            value = value + f32(got_z[(2 * step + q // 2) * 2 + q % 2])
        d_out[:, q * QUARTER : (q + 1) * QUARTER] = value.astype(jnp.bfloat16)

    for ring in firsts:
        ring.sent()
    for copy in later + z_copies:
        copy.wait_send()
    for m in range(4):
        owner = quarter * 4 + m

        @pl.when(owner != node)
        def _():
            pltpu.make_async_remote_copy(
                src_ref=g_part.at[:, pl.ds(32 * m, 32), :],
                dst_ref=got_g.at[sender],
                send_sem=g_send.at[m],
                recv_sem=g_recv.at[sender],
                device_id=(rel, owner),
                device_id_type=MESH,
            ).wait_send()


def reduce(d_part, g_part, adj, self_weight):
    dma = pltpu.SemaphoreType.DMA
    bf16 = jnp.bfloat16
    return pl.pallas_call(
        reduce_kernel,
        out_shape=(
            jax.ShapeDtypeStruct((2, 32, FEATURE), jnp.float32),
            jax.ShapeDtypeStruct((ROWS, FEATURE), bf16),
        ),
        in_specs=[VMEM, VMEM, ANY, ANY],
        out_specs=(VMEM, VMEM),
        scratch_shapes=[
            pltpu.VMEM((4, 6, 2, SIDE, ROWS, QUARTER), bf16),
            pltpu.VMEM((4, 2, 2, SIDE, ROWS, QUARTER), bf16),
            pltpu.VMEM((4, 3, 4, ROWS, QUARTER), bf16),
            pltpu.VMEM((4, 4, SIDE, ROWS, QUARTER), bf16),
            pltpu.VMEM((NODES, ROWS, QUARTER), bf16),
            pltpu.VMEM((NODES, ROWS, QUARTER), bf16),
            pltpu.VMEM((4, 2, 32, FEATURE), jnp.float32),
            pltpu.VMEM((ROWS, FEATURE), bf16),
            pltpu.VMEM((FEATURE, FEATURE), bf16),
            dma((2,)),
            dma((4, 6)),
            dma((4, 6)),
            dma((4, 3)),
            dma((4, 3)),
            dma((16,)),
            dma((16,)),
            dma((4,)),
            dma((4,)),
        ],
        compiler_params=pltpu.CompilerParams(
            collective_id=1, has_side_effects=True, vmem_limit_bytes=24 << 20
        ),
        name="sum_terms",
    )(d_part, g_part, adj, self_weight)


def on_device(
    out_adjoint,
    layer_input,
    rel_weights,
    self_weight,
    tile_values,
    tile_rel,
    tile_target,
    tile_src,
    tile_dest,
):
    code = (
        (tile_dest[:, :, 0] * BLOCKS + tile_src) * 2 + tile_rel
    ) * BLOCKS + tile_target
    meta = jnp.pad(code, ((0, 7), (0, 128 - TILES)))
    adj = out_adjoint[0]
    stay = functools.partial(
        pltpu.with_memory_space_constraint, memory_space=pltpu.HBM
    )
    tiles, a_rows, x_rows, codes = gather(
        stay(adj),
        stay(layer_input.reshape(SIDE, SIDE, ROWS, FEATURE)),
        stay(tile_values[0]),
        stay(meta),
    )
    d_part, g_part = local(
        stay(codes),
        tile_values[0],
        tiles.reshape(4 * TILES, EDGE, EDGE),
        a_rows.reshape(4 * BLOCKS, EDGE, FEATURE),
        x_rows.reshape(NODES * BLOCKS, EDGE, QUARTER),
        stay(rel_weights),
    )
    rel_weight_grad, d_source = reduce(
        d_part.reshape(NODES, SIDE, SIDE, ROWS, QUARTER), g_part, adj, self_weight
    )
    return rel_weight_grad, d_source[None]


def solution(mesh):
    return jax.shard_map(
        on_device,
        mesh=mesh,
        in_specs=(
            P("node", "rel", None),
            P("node", None, None),
            P("rel", None, None),
            P(),
            P("rel", "node", None, None),
            P("rel", "node"),
            P("rel", "node"),
            P("rel", "node"),
            P("rel", "node", None),
        ),
        out_specs=(P("rel", "node", None), P("node", "rel", None)),
        check_vma=False,
    )
```

```python
import functools

import jax
import jax.numpy as jnp
from jax import lax
from jax.experimental import pallas as pl
from jax.experimental.pallas import tpu as pltpu
from jax.sharding import PartitionSpec as P

MESH = pl.DeviceIdType.MESH
ANY = pl.BlockSpec(memory_space=pl.ANY)
VMEM = pl.BlockSpec(memory_space=pltpu.VMEM)
HBM = pl.BlockSpec(memory_space=pltpu.HBM)

SIDE = 4
NODES = 16
ROWS = 64
QUARTER = 128
TILES = 64
EDGE = 128
FEATURE = 512
BLOCKS = 8
CHUNK = 32


def place():
    rel, node = lax.axis_index("rel"), lax.axis_index("node")
    return (
        lax.div(rel, SIDE),
        lax.rem(rel, SIDE),
        lax.div(node, 2),
        lax.rem(node, 2),
        rel,
        node,
    )


def quarter_of(node):
    return lax.rem(lax.div(node, 2), 2) * 2 + lax.rem(node, 2)


def greet(x, y, rel, node):
    barrier = pltpu.get_barrier_semaphore()

    def call(there):
        pl.semaphore_signal(barrier, inc=1, device_id=there, device_id_type=MESH)

    for k in range(1, SIDE):
        call((lax.rem(x + k, SIDE) * SIDE + y, node))
        call((x * SIDE + lax.rem(y + k, SIDE), node))
    for k in range(1, NODES):
        call((rel, lax.rem(node + k, NODES)))
    pl.semaphore_wait(barrier, 2 * (SIDE - 1) + NODES - 1)


def push(src, dst, send, recv, there):
    copy = pltpu.make_async_remote_copy(
        src_ref=src,
        dst_ref=dst,
        send_sem=send,
        recv_sem=recv,
        device_id=there,
        device_id_type=MESH,
    )
    copy.start()
    return copy


def arrival(ref, sem):
    pltpu.make_async_copy(ref, ref, sem).wait()


class RingGather:
    def __init__(self, block, at, peer, send, recv):
        self.block, self.at, self.peer, self.send, self.recv = (
            block,
            at,
            peer,
            send,
            recv,
        )
        self.copies = []

    def move(self, view, number, k):
        self.copies.append(
            push(
                view,
                view,
                self.send.at[number],
                self.recv.at[number],
                self.peer(k),
            )
        )

    def place(self, k):
        return lax.rem(self.at + k, SIDE)

    def begin(self):
        mine = self.block(self.at, None)
        self.move(mine, 0, 1)
        self.move(mine, 1, SIDE - 1)

    def forward(self):
        arrival(self.block(self.place(3), None), self.recv.at[0])
        self.move(self.block(self.place(3), 0), 2, 1)
        arrival(self.block(self.place(1), None), self.recv.at[1])
        self.move(self.block(self.place(1), 1), 3, SIDE - 1)

    def finish(self):
        arrival(self.block(self.place(2), 0), self.recv.at[2])
        arrival(self.block(self.place(2), 1), self.recv.at[3])

    def sent(self):
        for copy in self.copies:
            copy.wait_send()


def gather_kernel(
    adj,
    layer,
    tiles,
    meta,
    t_all,
    a_all,
    x_all,
    m_all,
    local_sem,
    f_send,
    f_recv,
    a_send,
    a_recv,
    l_send,
    l_recv,
    x_send,
    x_recv,
    z_send,
    z_recv,
    t_send,
    t_recv,
    s_send,
    s_recv,
    m_send,
    m_recv,
):
    x, y, z, c, rel, node = place()
    half = ROWS // 2
    own = 1 + c
    near = 3 * c
    other = 2 - c
    sibling = (rel, z * 2 + (1 - c))
    beside = lax.rem(z + 7 + 2 * c, 8)
    away = 3 * (1 - c)
    halves = TILES // 2

    def x_peer(k):
        return (lax.rem(x + k, SIDE) * SIDE + y, node)

    def y_peer(k):
        return (x * SIDE + lax.rem(y + k, SIDE), node)

    every = slice(None)
    low, high = pl.ds(0, half), pl.ds(half, half)

    def part_of(h):
        return every if h is None else pl.ds(2 * h, 2)

    def second_leg(slot, number):
        return (
            RingGather(
                lambda p, h: a_all.at[slot, part_of(h), p, low],
                y,
                y_peer,
                a_send.at[number, 0],
                a_recv.at[number, 0],
            ),
            RingGather(
                lambda p, h: a_all.at[slot, p, part_of(h), high],
                x,
                x_peer,
                a_send.at[number, 1],
                a_recv.at[number, 1],
            ),
        )

    a_rings = (second_leg(own, 0), second_leg(near, 1))

    streams = ((2, 4, 2), (6, 4, 2), (10, 3, 2), (13, 3, 1))

    def x_view(stream, px, py, h):
        base, count, cut = streams[stream]
        shards = (pl.ds(base, cut), pl.ds(base + cut, count - cut))
        return x_all.at[pl.ds(base, count) if h is None else shards[h], px, py]

    def second_x(stream):
        if stream % 2 == 1:
            return RingGather(
                lambda p, h: x_view(stream, p, every, h),
                x,
                x_peer,
                x_send.at[stream],
                x_recv.at[stream],
            )
        return RingGather(
            lambda p, h: x_view(stream, every, p, h),
            y,
            y_peer,
            x_send.at[stream],
            x_recv.at[stream],
        )

    x_rings = [second_x(stream) for stream in range(4)]

    greet(x, y, rel, node)

    a_near = push(
        adj,
        a_all.at[away, x, y],
        t_send.at[2],
        t_recv.at[2],
        (rel, beside * 2 + 1 - c),
    )

    a_first = ([], [])

    def a_send_first(source, slot, number):
        for k in range(1, SIDE):
            for rows, peer, stream in ((low, x_peer, 0), (high, y_peer, 1)):
                at = (number, stream, k - 1)
                a_first[number].append(
                    push(
                        source.at[rows],
                        a_all.at[slot, x, y, rows],
                        f_send.at[at],
                        f_recv.at[at],
                        peer(k),
                    )
                )

    a_send_first(adj, own, 0)
    a_own = pltpu.make_async_copy(adj, a_all.at[own, x, y], local_sem.at[0])
    a_own.start()

    def columns(there):
        return pl.ds(pl.multiple_of(quarter_of(there) * QUARTER, QUARTER), QUARTER)

    z_copies = []
    for k in (1, 7, 2, 6, 3, 5, 4):
        for core in range(2):
            there = lax.rem(z + k, 8) * 2 + core
            index = (8 - k) * 2 + c
            z_copies.append(
                push(
                    layer.at[x, y, :, columns(there)],
                    x_all.at[index, x, y],
                    z_send.at[2 * k + core - 2],
                    z_recv.at[index - 2],
                    (rel, there),
                )
            )

    arrival(a_all.at[near, x, y], t_recv.at[2])
    a_send_first(a_all.at[near, x, y], near, 1)

    t_near = push(tiles, t_all.at[own], s_send.at[0], s_recv.at[0], sibling)
    m_copies = [push(meta, m_all.at[own], m_send.at[0], m_recv.at[0], sibling)]
    for h in range(2):
        m_copies.append(
            push(
                meta,
                m_all.at[away],
                m_send.at[1 + h],
                m_recv.at[1 + c],
                (rel, beside * 2 + h),
            )
        )
    m_own = pltpu.make_async_copy(meta, m_all.at[own], local_sem.at[2])
    m_own.start()

    x_near = push(
        layer.at[:, :, :, columns(z * 2 + 1 - c)],
        x_all.at[c],
        s_send.at[4],
        s_recv.at[4],
        sibling,
    )
    x_own = pltpu.make_async_copy(
        layer.at[:, :, :, columns(node)], x_all.at[c], local_sem.at[1]
    )
    x_own.start()

    a_own.wait()
    for number in range(2):
        for copy in a_first[number]:
            copy.wait_recv()
        for ring in a_rings[number]:
            ring.begin()

    t_far = []
    for h in range(2):
        part = pl.ds(h * halves, halves)
        t_far.append(
            push(
                tiles.at[part],
                t_all.at[away, part],
                t_send.at[h],
                t_recv.at[c],
                (rel, beside * 2 + h),
            )
        )
    x_first = [[] for _ in streams]
    for stream in range(4):
        base, count, _ = streams[stream]
        for index in range(base, base + count):
            arrival(x_all.at[index, x, y], z_recv.at[index - 2])
        mine = x_view(stream, x, y, None)
        for k in (2, 1, 3):
            x_first[stream].append(
                push(
                    mine,
                    mine,
                    l_send.at[stream, k - 1],
                    l_recv.at[stream, k - 1],
                    (x_peer if stream % 2 == 0 else y_peer)(k),
                )
            )
    for ring in a_rings[0] + a_rings[1]:
        ring.forward()
    for stream in range(4):
        for copy in x_first[stream]:
            copy.wait_recv()
        x_rings[stream].begin()
    for ring in a_rings[0] + a_rings[1]:
        ring.finish()
    pair = pl.ds(2 * c, 2)
    a_over = push(a_all.at[pair], a_all.at[pair], s_send.at[1], s_recv.at[1], sibling)
    for stream in range(4):
        x_rings[stream].forward()

    onward = []
    mine = pl.ds(c * halves, halves)
    for sender, slot in ((0, 3), (1, 0)):
        arrival(t_all.at[slot, mine], t_recv.at[sender])
        onward.append(
            push(
                t_all.at[slot, mine],
                t_all.at[slot, mine],
                s_send.at[2 + sender],
                s_recv.at[2 + sender],
                sibling,
            )
        )
    for stream in range(4):
        x_rings[stream].finish()

    arrival(t_all.at[other], s_recv.at[0])
    arrival(a_all.at[pl.ds(2 - 2 * c, 2)], s_recv.at[1])
    theirs = pl.ds((1 - c) * halves, halves)
    for sender, slot in ((0, 3), (1, 0)):
        arrival(t_all.at[slot, theirs], s_recv.at[2 + sender])
    arrival(m_all.at[other], m_recv.at[0])
    arrival(m_all.at[3], m_recv.at[1])
    arrival(m_all.at[0], m_recv.at[2])
    m_own.wait()
    x_own.wait()
    arrival(x_all.at[1 - c], s_recv.at[4])
    for ring in a_rings[0] + a_rings[1]:
        ring.sent()
    for ring in x_rings:
        ring.sent()
    for copies in x_first:
        for copy in copies:
            copy.wait_send()
    for copy in (
        [a_near, t_near, a_over, x_near]
        + a_first[0]
        + a_first[1]
        + z_copies
        + m_copies
        + t_far
        + onward
    ):
        copy.wait_send()


def gather(adj, layer, tiles, meta):
    dma = pltpu.SemaphoreType.DMA
    return pl.pallas_call(
        gather_kernel,
        out_shape=(
            jax.ShapeDtypeStruct((4, TILES, EDGE, EDGE), jnp.bfloat16),
            jax.ShapeDtypeStruct((4, SIDE, SIDE, ROWS, FEATURE), jnp.bfloat16),
            jax.ShapeDtypeStruct((NODES, SIDE, SIDE, ROWS, QUARTER), jnp.bfloat16),
            jax.ShapeDtypeStruct((4, 8, TILES), jnp.int32),
        ),
        in_specs=[ANY] * 4,
        out_specs=(VMEM, VMEM, VMEM, ANY),
        scratch_shapes=[
            dma((3,)),
            dma((2, 2, 3)),
            dma((2, 2, 3)),
            dma((2, 2, 4)),
            dma((2, 2, 4)),
            dma((4, 3)),
            dma((4, 3)),
            dma((4, 4)),
            dma((4, 4)),
            dma((14,)),
            dma((14,)),
            dma((3,)),
            dma((3,)),
            dma((5,)),
            dma((5,)),
            dma((3,)),
            dma((3,)),
        ],
        compiler_params=pltpu.CompilerParams(
            collective_id=0, has_side_effects=True, vmem_limit_bytes=24 << 20
        ),
        cost_estimate=pl.CostEstimate(
            flops=0, bytes_accessed=32 << 20, transcendentals=0
        ),
        name="gather_rows_and_tiles",
    )(adj, layer, tiles, meta)


def local_kernel(
    meta_in,
    own_tiles,
    tiles,
    a_rows,
    x_rows,
    weights_in,
    d_out,
    g_out,
    weights,
    aw,
    d_sum,
    h_sum,
    h_turned,
    meta,
    in_sem,
):
    quarter = quarter_of(lax.axis_index("node"))
    shards = 4
    buckets = NODES * BLOCKS
    width = 4 * EDGE
    column = pl.multiple_of(quarter * QUARTER, QUARTER)

    def fetch(src, dst, sem):
        copy = pltpu.make_async_copy(src, dst, sem)
        copy.start()
        return copy

    get_meta = fetch(meta_in, meta, in_sem.at[0])
    get_w = fetch(weights_in.at[:, pl.ds(column, QUARTER)], weights, in_sem.at[1])
    core = lax.rem(lax.axis_index("node"), 2)
    chip = lax.div(lax.axis_index("node"), 2)
    each = TILES // CHUNK

    d_sum[...] = jnp.zeros_like(d_sum)
    h_sum[...] = jnp.zeros_like(h_sum)

    get_w.wait()
    both = weights[...].reshape(2 * QUARTER, FEATURE)
    for b in range(shards * BLOCKS // 4):
        rows = a_rows[pl.ds(b * 4, 4)].reshape(width, FEATURE)
        value = lax.dot_general(
            both,
            rows,
            (((1,), (1,)), ((), ())),
            preferred_element_type=jnp.float32,
        ).astype(jnp.bfloat16)
        for r in range(2):
            for i in range(4):
                aw[r, b * 4 + i] = value[
                    r * QUARTER : (r + 1) * QUARTER, i * EDGE : (i + 1) * EDGE
                ]
    get_meta.wait()

    def some(n, source, start):
        slot = lax.div(n * CHUNK, TILES)
        first = lax.rem(n * CHUNK, TILES)
        for k in range(CHUNK):
            code = meta[slot, 0, first + k]
            target = slot * BLOCKS + lax.rem(code, BLOCKS)
            relation = lax.rem(lax.div(code, BLOCKS), 2)
            bucket = jnp.bitwise_and(
                lax.div(code, 2 * BLOCKS) - 16 * chip, buckets - 1
            )
            tile = source[start + k]
            d_sum[bucket] += jnp.dot(
                aw[relation, target], tile, preferred_element_type=jnp.float32
            )
            h_sum[relation, target] += jnp.dot(
                tile, x_rows[bucket], preferred_element_type=jnp.float32
            )

    def own_some(i, carry):
        some((1 + core) * each + i, own_tiles, i * CHUNK)
        return carry

    def other_some(i, carry):
        number = lax.div(i, each)
        slot = lax.rem(4 - core * lax.rem(number, 2) + 2 * lax.rem(number, 2), 4)
        slot = jnp.where(number == 2, 3, slot)
        n = slot * each + lax.rem(i, each)
        some(n, tiles, n * CHUNK)
        return carry

    lax.fori_loop(0, each, own_some, 0)
    lax.fori_loop(0, 3 * each, other_some, 0)

    def turn(n, carry):
        for k in range(16):
            d_out[n * 16 + k] = d_sum[n * 16 + k].astype(jnp.bfloat16).T
        return carry

    lax.fori_loop(0, buckets // 16, turn, 0)
    for r in range(2):
        for b in range(shards * BLOCKS):
            h_turned[:, pl.ds(b * EDGE, EDGE)] = h_sum[r, b].astype(jnp.bfloat16).T
        g_out[r] = jnp.dot(
            h_turned[...],
            a_rows[...].reshape(shards * BLOCKS * EDGE, FEATURE),
            preferred_element_type=jnp.float32,
        )


def local(meta, own_tiles, tiles, a_rows, x_rows, weights):
    buckets = NODES * BLOCKS
    shards = 4
    bf16 = jnp.bfloat16
    return pl.pallas_call(
        local_kernel,
        out_shape=(
            jax.ShapeDtypeStruct((buckets, EDGE, QUARTER), bf16),
            jax.ShapeDtypeStruct((2, QUARTER, FEATURE), jnp.float32),
        ),
        in_specs=[ANY, VMEM, VMEM, VMEM, VMEM, HBM],
        out_specs=(VMEM, VMEM),
        scratch_shapes=[
            pltpu.VMEM((2, QUARTER, FEATURE), bf16),
            pltpu.VMEM((2, shards * BLOCKS, QUARTER, EDGE), bf16),
            pltpu.VMEM((buckets, QUARTER, EDGE), jnp.float32),
            pltpu.VMEM((2, shards * BLOCKS, EDGE, QUARTER), jnp.float32),
            pltpu.VMEM((QUARTER, shards * BLOCKS * EDGE), bf16),
            pltpu.SMEM((shards, 8, TILES), jnp.int32),
            pltpu.SemaphoreType.DMA((2,)),
        ],
        compiler_params=pltpu.CompilerParams(vmem_limit_bytes=24 << 20),
        name="tile_products",
    )(meta, own_tiles, tiles, a_rows, x_rows, weights)


class RingSum:
    def __init__(self, term, send_term, at, peer, got, out, send, recv):
        self.term, self.send_term, self.at, self.peer = term, send_term, at, peer
        self.got, self.out, self.send, self.recv = got, out, send, recv
        self.copies = []

    def place(self, k):
        return lax.rem(self.at + k, SIDE)

    def move(self, view, number, k):
        self.copies.append(
            push(
                view,
                self.got.at[number],
                self.send.at[number],
                self.recv.at[number],
                self.peer(k),
            )
        )

    def begin(self):
        self.move(self.send_term(self.place(2), 0), 0, SIDE - 1)
        self.move(self.send_term(self.place(2), 1), 1, 1)

    def direct(self):
        self.move(self.send_term(self.place(1), 0), 2, 1)
        self.move(self.send_term(self.place(3), 1), 3, SIDE - 1)

    def pass_on(self):
        for number, k, h in ((0, SIDE - 1, 0), (1, 1, 1)):
            arrival(self.got.at[number], self.recv.at[number])
            value = f32(self.term(self.place(k), h)[...]) + f32(self.got[number])
            self.out[h] = value.astype(jnp.bfloat16)
            self.move(self.out.at[h], 4 + h, k)

    def result(self, h):
        for number in (2 + h, 4 + h):
            arrival(self.got.at[number], self.recv.at[number])
        value = f32(self.got[2 + h]) + f32(self.got[4 + h])
        return (value + f32(self.term(self.at, h)[...])).astype(jnp.bfloat16)

    def sent(self):
        for copy in self.copies:
            copy.wait_send()


def f32(value):
    return value.astype(jnp.float32)


def reduce_kernel(
    d_part,
    g_part,
    adj_in,
    self_weight_in,
    g_out,
    d_out,
    got_first,
    out_first,
    got_second,
    summed,
    total,
    got_z,
    got_g,
    adj,
    self_weight,
    local_sem,
    r_send,
    r_recv,
    q_send,
    q_recv,
    z_send,
    z_recv,
    g_send,
    g_recv,
):
    x, y, z, c, rel, node = place()
    quarter = quarter_of(node)
    streams = 4

    def x_peer(k):
        return (lax.rem(x + k, SIDE) * SIDE + y, node)

    def y_peer(k):
        return (x * SIDE + lax.rem(y + k, SIDE), node)

    def fetch(src, dst, sem):
        copy = pltpu.make_async_copy(src, dst, sem)
        copy.start()
        return copy

    get_adj = fetch(adj_in, adj, local_sem.at[0])
    get_weight = fetch(self_weight_in, self_weight, local_sem.at[1])

    def first_ring(stream):
        along_x = stream % 2 == 0

        def view(ref, p, h):
            shards = pl.ds(4 * stream + 2 * h, 2)
            return ref.at[shards, p] if along_x else ref.at[shards, :, p]

        return RingSum(
            lambda p, h: view(d_part, p, h),
            lambda p, h: view(d_part, p, h),
            x if along_x else y,
            x_peer if along_x else y_peer,
            got_first.at[stream],
            out_first.at[stream],
            r_send.at[stream],
            r_recv.at[stream],
        )

    firsts = [first_ring(stream) for stream in range(streams)]

    greet(x, y, rel, node)

    for ring in firsts:
        ring.begin()
    for ring in firsts:
        ring.direct()

    sender = lax.div(z, 2)
    for m in range(4):
        owner = quarter * 4 + m
        rows = g_part.at[:, pl.ds(32 * m, 32), :]

        @pl.when(owner != node)
        def _():
            push(
                rows,
                got_g.at[sender],
                g_send.at[m],
                g_recv.at[sender],
                (rel, owner),
            )

        @pl.when(owner == node)
        def _():
            pltpu.make_async_copy(rows, got_g.at[sender], g_recv.at[sender]).start()

    later = []

    def middle(stream):
        for h in range(2):
            summed[stream, pl.ds(2 * h, 2)] = firsts[stream].result(h)
        at, peer = (y, y_peer) if stream % 2 == 0 else (x, x_peer)
        for k in (2, 1, 3):
            later.append(
                push(
                    summed.at[stream, :, lax.rem(at + k, SIDE)],
                    got_second.at[stream, k - 1],
                    q_send.at[stream, k - 1],
                    q_recv.at[stream, k - 1],
                    peer(k),
                )
            )

    z_copies = []

    def last(stream):
        for k in range(SIDE - 1):
            arrival(got_second.at[stream, k], q_recv.at[stream, k])
        value = f32(summed[stream, :, y if stream % 2 == 0 else x])
        for k in range(SIDE - 1):
            value = value + f32(got_second[stream, k])
        total[pl.ds(4 * stream, 4)] = value.astype(jnp.bfloat16)
        for up in (2 * stream, 2 * stream + 1):
            cores = (1 - c,) if up == 0 else (0, 1)
            for number, core in enumerate(cores):
                z_copies.append(
                    push(
                        total.at[2 * up + core],
                        got_z.at[node],
                        z_send.at[2 * up + number],
                        z_recv.at[2 * up + c],
                        (rel, lax.rem(z + up, 8) * 2 + core),
                    )
                )
        if stream == 0:
            got_z[node] = total[c]

    for ring in firsts:
        ring.pass_on()
    middle(0)
    middle(1)
    middle(2)
    middle(3)
    last(0)
    last(1)
    last(2)
    last(3)

    get_adj.wait()
    get_weight.wait()
    own_term = lax.dot_general(
        adj[...],
        self_weight[...],
        (((1,), (1,)), ((), ())),
        preferred_element_type=jnp.float32,
    )

    for m in range(4):
        arrival(got_g.at[m], g_recv.at[m])
    g_out[...] = (got_g[0] + got_g[1]) + (got_g[2] + got_g[3])

    arrival(got_z.at[z * 2 + 1 - c], z_recv.at[1 - c])
    for up in range(1, 8):
        for core in range(2):
            arrival(
                got_z.at[lax.rem(z + 8 - up, 8) * 2 + core], z_recv.at[2 * up + core]
            )
    for q in range(4):
        value = own_term[:, q * QUARTER : (q + 1) * QUARTER]
        for step in range(4):
            value = value + f32(got_z[(2 * step + q // 2) * 2 + q % 2])
        d_out[:, q * QUARTER : (q + 1) * QUARTER] = value.astype(jnp.bfloat16)

    for ring in firsts:
        ring.sent()
    for copy in later + z_copies:
        copy.wait_send()
    for m in range(4):
        owner = quarter * 4 + m

        @pl.when(owner != node)
        def _():
            pltpu.make_async_remote_copy(
                src_ref=g_part.at[:, pl.ds(32 * m, 32), :],
                dst_ref=got_g.at[sender],
                send_sem=g_send.at[m],
                recv_sem=g_recv.at[sender],
                device_id=(rel, owner),
                device_id_type=MESH,
            ).wait_send()


def reduce(d_part, g_part, adj, self_weight):
    dma = pltpu.SemaphoreType.DMA
    bf16 = jnp.bfloat16
    return pl.pallas_call(
        reduce_kernel,
        out_shape=(
            jax.ShapeDtypeStruct((2, 32, FEATURE), jnp.float32),
            jax.ShapeDtypeStruct((ROWS, FEATURE), bf16),
        ),
        in_specs=[VMEM, VMEM, ANY, ANY],
        out_specs=(VMEM, VMEM),
        scratch_shapes=[
            pltpu.VMEM((4, 6, 2, SIDE, ROWS, QUARTER), bf16),
            pltpu.VMEM((4, 2, 2, SIDE, ROWS, QUARTER), bf16),
            pltpu.VMEM((4, 3, 4, ROWS, QUARTER), bf16),
            pltpu.VMEM((4, 4, SIDE, ROWS, QUARTER), bf16),
            pltpu.VMEM((NODES, ROWS, QUARTER), bf16),
            pltpu.VMEM((NODES, ROWS, QUARTER), bf16),
            pltpu.VMEM((4, 2, 32, FEATURE), jnp.float32),
            pltpu.VMEM((ROWS, FEATURE), bf16),
            pltpu.VMEM((FEATURE, FEATURE), bf16),
            dma((2,)),
            dma((4, 6)),
            dma((4, 6)),
            dma((4, 3)),
            dma((4, 3)),
            dma((16,)),
            dma((16,)),
            dma((4,)),
            dma((4,)),
        ],
        compiler_params=pltpu.CompilerParams(
            collective_id=1, has_side_effects=True, vmem_limit_bytes=24 << 20
        ),
        name="sum_terms",
    )(d_part, g_part, adj, self_weight)


def on_device(
    out_adjoint,
    layer_input,
    rel_weights,
    self_weight,
    tile_values,
    tile_rel,
    tile_target,
    tile_src,
    tile_dest,
):
    code = (
        (tile_dest[:, :, 0] * BLOCKS + tile_src) * 2 + tile_rel
    ) * BLOCKS + tile_target
    meta = jnp.broadcast_to(code, (8, TILES))
    adj = out_adjoint[0]
    stay = functools.partial(
        pltpu.with_memory_space_constraint, memory_space=pltpu.HBM
    )
    tiles, a_rows, x_rows, codes = gather(
        stay(adj),
        stay(layer_input.reshape(SIDE, SIDE, ROWS, FEATURE)),
        stay(tile_values[0]),
        stay(meta),
    )
    d_part, g_part = local(
        codes,
        tile_values[0],
        tiles.reshape(4 * TILES, EDGE, EDGE),
        a_rows.reshape(4 * BLOCKS, EDGE, FEATURE),
        x_rows.reshape(NODES * BLOCKS, EDGE, QUARTER),
        stay(rel_weights),
    )
    rel_weight_grad, d_source = reduce(
        d_part.reshape(NODES, SIDE, SIDE, ROWS, QUARTER), g_part, adj, self_weight
    )
    return rel_weight_grad, d_source[None]


def solution(mesh):
    return jax.shard_map(
        on_device,
        mesh=mesh,
        in_specs=(
            P("node", "rel", None),
            P("node", None, None),
            P("rel", None, None),
            P(),
            P("rel", "node", None, None),
            P("rel", "node"),
            P("rel", "node"),
            P("rel", "node"),
            P("rel", "node", None),
        ),
        out_specs=(P("rel", "node", None), P("node", "rel", None)),
        check_vma=False,
    )
```

```python
import functools

import jax
import jax.numpy as jnp
from jax import lax
from jax.experimental import pallas as pl
from jax.experimental.pallas import tpu as pltpu
from jax.sharding import PartitionSpec as P

MESH = pl.DeviceIdType.MESH
ANY = pl.BlockSpec(memory_space=pl.ANY)
VMEM = pl.BlockSpec(memory_space=pltpu.VMEM)
HBM = pl.BlockSpec(memory_space=pltpu.HBM)

SIDE = 4
NODES = 16
ROWS = 64
QUARTER = 128
TILES = 64
EDGE = 128
FEATURE = 512
BLOCKS = 8
CHUNK = 32


def place():
    rel, node = lax.axis_index("rel"), lax.axis_index("node")
    return (
        lax.div(rel, SIDE),
        lax.rem(rel, SIDE),
        lax.div(node, 2),
        lax.rem(node, 2),
        rel,
        node,
    )


def quarter_of(node):
    return lax.rem(lax.div(node, 2), 2) * 2 + lax.rem(node, 2)


def greet(x, y, rel, node):
    barrier = pltpu.get_barrier_semaphore()

    def call(there):
        pl.semaphore_signal(barrier, inc=1, device_id=there, device_id_type=MESH)

    for k in range(1, SIDE):
        call((lax.rem(x + k, SIDE) * SIDE + y, node))
        call((x * SIDE + lax.rem(y + k, SIDE), node))
    for k in range(1, NODES):
        call((rel, lax.rem(node + k, NODES)))
    pl.semaphore_wait(barrier, 2 * (SIDE - 1) + NODES - 1)


def push(src, dst, send, recv, there):
    copy = pltpu.make_async_remote_copy(
        src_ref=src,
        dst_ref=dst,
        send_sem=send,
        recv_sem=recv,
        device_id=there,
        device_id_type=MESH,
    )
    copy.start()
    return copy


def arrival(ref, sem):
    pltpu.make_async_copy(ref, ref, sem).wait()


class RingGather:
    def __init__(self, block, at, peer, send, recv):
        self.block, self.at, self.peer, self.send, self.recv = (
            block,
            at,
            peer,
            send,
            recv,
        )
        self.copies = []

    def move(self, view, number, k):
        self.copies.append(
            push(
                view,
                view,
                self.send.at[number],
                self.recv.at[number],
                self.peer(k),
            )
        )

    def place(self, k):
        return lax.rem(self.at + k, SIDE)

    def begin(self):
        mine = self.block(self.at, None)
        self.move(mine, 0, 1)
        self.move(mine, 1, SIDE - 1)

    def forward(self):
        arrival(self.block(self.place(3), None), self.recv.at[0])
        self.move(self.block(self.place(3), 0), 2, 1)
        arrival(self.block(self.place(1), None), self.recv.at[1])
        self.move(self.block(self.place(1), 1), 3, SIDE - 1)

    def finish(self):
        arrival(self.block(self.place(2), 0), self.recv.at[2])
        arrival(self.block(self.place(2), 1), self.recv.at[3])

    def sent(self):
        for copy in self.copies:
            copy.wait_send()


def gather_kernel(
    adj,
    layer,
    tiles,
    meta,
    t_all,
    a_all,
    x_all,
    m_all,
    local_sem,
    f_send,
    f_recv,
    a_send,
    a_recv,
    l_send,
    l_recv,
    x_send,
    x_recv,
    z_send,
    z_recv,
    t_send,
    t_recv,
    s_send,
    s_recv,
    m_send,
    m_recv,
):
    x, y, z, c, rel, node = place()
    half = ROWS // 2
    own = 1 + c
    near = 3 * c
    other = 2 - c
    sibling = (rel, z * 2 + (1 - c))
    beside = lax.rem(z + 7 + 2 * c, 8)
    away = 3 * (1 - c)
    halves = TILES // 2

    def x_peer(k):
        return (lax.rem(x + k, SIDE) * SIDE + y, node)

    def y_peer(k):
        return (x * SIDE + lax.rem(y + k, SIDE), node)

    every = slice(None)
    low, high = pl.ds(0, half), pl.ds(half, half)

    def part_of(h):
        return every if h is None else pl.ds(2 * h, 2)

    def second_leg(slot, number):
        return (
            RingGather(
                lambda p, h: a_all.at[slot, part_of(h), p, low],
                y,
                y_peer,
                a_send.at[number, 0],
                a_recv.at[number, 0],
            ),
            RingGather(
                lambda p, h: a_all.at[slot, p, part_of(h), high],
                x,
                x_peer,
                a_send.at[number, 1],
                a_recv.at[number, 1],
            ),
        )

    a_rings = (second_leg(own, 0), second_leg(near, 1))

    streams = ((2, 4, 2), (6, 4, 2), (10, 3, 2), (13, 3, 1))

    def x_view(stream, px, py, h):
        base, count, cut = streams[stream]
        shards = (pl.ds(base, cut), pl.ds(base + cut, count - cut))
        return x_all.at[pl.ds(base, count) if h is None else shards[h], px, py]

    def second_x(stream):
        if stream % 2 == 1:
            return RingGather(
                lambda p, h: x_view(stream, p, every, h),
                x,
                x_peer,
                x_send.at[stream],
                x_recv.at[stream],
            )
        return RingGather(
            lambda p, h: x_view(stream, every, p, h),
            y,
            y_peer,
            x_send.at[stream],
            x_recv.at[stream],
        )

    x_rings = [second_x(stream) for stream in range(4)]

    greet(x, y, rel, node)

    a_near = push(
        adj,
        a_all.at[away, x, y],
        t_send.at[2],
        t_recv.at[2],
        (rel, beside * 2 + 1 - c),
    )

    a_first = ([], [])

    def a_send_first(source, slot, number):
        for k in range(1, SIDE):
            for rows, peer, stream in ((low, x_peer, 0), (high, y_peer, 1)):
                at = (number, stream, k - 1)
                a_first[number].append(
                    push(
                        source.at[rows],
                        a_all.at[slot, x, y, rows],
                        f_send.at[at],
                        f_recv.at[at],
                        peer(k),
                    )
                )

    a_send_first(adj, own, 0)
    a_own = pltpu.make_async_copy(adj, a_all.at[own, x, y], local_sem.at[0])
    a_own.start()

    def columns(there):
        return pl.ds(pl.multiple_of(quarter_of(there) * QUARTER, QUARTER), QUARTER)

    z_copies = []
    for k in (1, 7, 2, 6, 3, 5, 4):
        for core in range(2):
            there = lax.rem(z + k, 8) * 2 + core
            index = (8 - k) * 2 + c
            z_copies.append(
                push(
                    layer.at[x, y, :, columns(there)],
                    x_all.at[index, x, y],
                    z_send.at[2 * k + core - 2],
                    z_recv.at[index - 2],
                    (rel, there),
                )
            )

    t_far = []
    for h in range(2):
        part = pl.ds(h * halves, halves)
        t_far.append(
            push(
                tiles.at[part],
                t_all.at[away, part],
                t_send.at[h],
                t_recv.at[c],
                (rel, beside * 2 + h),
            )
        )
    arrival(a_all.at[near, x, y], t_recv.at[2])
    a_send_first(a_all.at[near, x, y], near, 1)

    t_near = push(tiles, t_all.at[own], s_send.at[0], s_recv.at[0], sibling)
    m_copies = [push(meta, m_all.at[own], m_send.at[0], m_recv.at[0], sibling)]
    for h in range(2):
        m_copies.append(
            push(
                meta,
                m_all.at[away],
                m_send.at[1 + h],
                m_recv.at[1 + c],
                (rel, beside * 2 + h),
            )
        )
    m_own = pltpu.make_async_copy(meta, m_all.at[own], local_sem.at[2])
    m_own.start()

    x_near = push(
        layer.at[:, :, :, columns(z * 2 + 1 - c)],
        x_all.at[c],
        s_send.at[4],
        s_recv.at[4],
        sibling,
    )
    x_own = pltpu.make_async_copy(
        layer.at[:, :, :, columns(node)], x_all.at[c], local_sem.at[1]
    )
    x_own.start()

    a_own.wait()
    for number in range(2):
        for copy in a_first[number]:
            copy.wait_recv()
        for ring in a_rings[number]:
            ring.begin()

    x_first = [[] for _ in streams]
    for stream in range(4):
        base, count, _ = streams[stream]
        for index in range(base, base + count):
            arrival(x_all.at[index, x, y], z_recv.at[index - 2])
        mine = x_view(stream, x, y, None)
        for k in (2, 1, 3):
            x_first[stream].append(
                push(
                    mine,
                    mine,
                    l_send.at[stream, k - 1],
                    l_recv.at[stream, k - 1],
                    (x_peer if stream % 2 == 0 else y_peer)(k),
                )
            )
    for ring in a_rings[0] + a_rings[1]:
        ring.forward()
    for stream in range(4):
        for copy in x_first[stream]:
            copy.wait_recv()
        x_rings[stream].begin()
    for ring in a_rings[0] + a_rings[1]:
        ring.finish()
    pair = pl.ds(2 * c, 2)
    a_over = push(a_all.at[pair], a_all.at[pair], s_send.at[1], s_recv.at[1], sibling)
    for stream in range(4):
        x_rings[stream].forward()

    onward = []
    mine = pl.ds(c * halves, halves)
    for sender, slot in ((0, 3), (1, 0)):
        arrival(t_all.at[slot, mine], t_recv.at[sender])
        onward.append(
            push(
                t_all.at[slot, mine],
                t_all.at[slot, mine],
                s_send.at[2 + sender],
                s_recv.at[2 + sender],
                sibling,
            )
        )
    for stream in range(4):
        x_rings[stream].finish()

    arrival(t_all.at[other], s_recv.at[0])
    arrival(a_all.at[pl.ds(2 - 2 * c, 2)], s_recv.at[1])
    theirs = pl.ds((1 - c) * halves, halves)
    for sender, slot in ((0, 3), (1, 0)):
        arrival(t_all.at[slot, theirs], s_recv.at[2 + sender])
    arrival(m_all.at[other], m_recv.at[0])
    arrival(m_all.at[3], m_recv.at[1])
    arrival(m_all.at[0], m_recv.at[2])
    m_own.wait()
    x_own.wait()
    arrival(x_all.at[1 - c], s_recv.at[4])
    for ring in a_rings[0] + a_rings[1]:
        ring.sent()
    for ring in x_rings:
        ring.sent()
    for copies in x_first:
        for copy in copies:
            copy.wait_send()
    for copy in (
        [a_near, t_near, a_over, x_near]
        + a_first[0]
        + a_first[1]
        + z_copies
        + m_copies
        + t_far
        + onward
    ):
        copy.wait_send()


def gather(adj, layer, tiles, meta):
    dma = pltpu.SemaphoreType.DMA
    return pl.pallas_call(
        gather_kernel,
        out_shape=(
            jax.ShapeDtypeStruct((4, TILES, EDGE, EDGE), jnp.bfloat16),
            jax.ShapeDtypeStruct((4, SIDE, SIDE, ROWS, FEATURE), jnp.bfloat16),
            jax.ShapeDtypeStruct((NODES, SIDE, SIDE, ROWS, QUARTER), jnp.bfloat16),
            jax.ShapeDtypeStruct((4, 8, TILES), jnp.int32),
        ),
        in_specs=[ANY] * 4,
        out_specs=(VMEM, VMEM, VMEM, ANY),
        scratch_shapes=[
            dma((3,)),
            dma((2, 2, 3)),
            dma((2, 2, 3)),
            dma((2, 2, 4)),
            dma((2, 2, 4)),
            dma((4, 3)),
            dma((4, 3)),
            dma((4, 4)),
            dma((4, 4)),
            dma((14,)),
            dma((14,)),
            dma((3,)),
            dma((3,)),
            dma((5,)),
            dma((5,)),
            dma((3,)),
            dma((3,)),
        ],
        compiler_params=pltpu.CompilerParams(
            collective_id=0, has_side_effects=True, vmem_limit_bytes=24 << 20
        ),
        cost_estimate=pl.CostEstimate(
            flops=0, bytes_accessed=32 << 20, transcendentals=0
        ),
        name="gather_rows_and_tiles",
    )(adj, layer, tiles, meta)


def local_kernel(
    meta_in,
    own_tiles,
    tiles,
    a_rows,
    x_rows,
    weights_in,
    d_out,
    g_out,
    weights,
    aw,
    d_sum,
    h_sum,
    h_turned,
    meta,
    in_sem,
):
    quarter = quarter_of(lax.axis_index("node"))
    shards = 4
    buckets = NODES * BLOCKS
    width = 4 * EDGE
    column = pl.multiple_of(quarter * QUARTER, QUARTER)

    def fetch(src, dst, sem):
        copy = pltpu.make_async_copy(src, dst, sem)
        copy.start()
        return copy

    get_meta = fetch(meta_in, meta, in_sem.at[0])
    get_w = fetch(weights_in.at[:, pl.ds(column, QUARTER)], weights, in_sem.at[1])
    core = lax.rem(lax.axis_index("node"), 2)
    chip = lax.div(lax.axis_index("node"), 2)
    each = TILES // CHUNK

    d_sum[...] = jnp.zeros_like(d_sum)
    h_sum[...] = jnp.zeros_like(h_sum)

    get_w.wait()
    both = weights[...].reshape(2 * QUARTER, FEATURE)
    for b in range(shards * BLOCKS // 4):
        rows = a_rows[pl.ds(b * 4, 4)].reshape(width, FEATURE)
        value = lax.dot_general(
            both,
            rows,
            (((1,), (1,)), ((), ())),
            preferred_element_type=jnp.float32,
        ).astype(jnp.bfloat16)
        for r in range(2):
            for i in range(4):
                aw[r, b * 4 + i] = value[
                    r * QUARTER : (r + 1) * QUARTER, i * EDGE : (i + 1) * EDGE
                ]
    get_meta.wait()

    def some(n, source, start):
        slot = lax.div(n * CHUNK, TILES)
        first = lax.rem(n * CHUNK, TILES)
        for k in range(CHUNK):
            code = meta[slot, 0, first + k]
            target = slot * BLOCKS + lax.rem(code, BLOCKS)
            relation = lax.rem(lax.div(code, BLOCKS), 2)
            bucket = jnp.bitwise_and(
                lax.div(code, 2 * BLOCKS) - 16 * chip, buckets - 1
            )
            tile = source[start + k]
            d_sum[bucket] += jnp.dot(
                aw[relation, target], tile, preferred_element_type=jnp.float32
            )
            h_sum[relation, target] += jnp.dot(
                tile, x_rows[bucket], preferred_element_type=jnp.float32
            )

    def own_some(i, carry):
        some((1 + core) * each + i, own_tiles, i * CHUNK)
        return carry

    def other_some(i, carry):
        number = lax.div(i, each)
        slot = lax.rem(4 - core * lax.rem(number, 2) + 2 * lax.rem(number, 2), 4)
        slot = jnp.where(number == 2, 3, slot)
        n = slot * each + lax.rem(i, each)
        some(n, tiles, n * CHUNK)
        return carry

    lax.fori_loop(0, each, own_some, 0)
    lax.fori_loop(0, 3 * each, other_some, 0)

    def turn(n, carry):
        for k in range(16):
            d_out[n * 16 + k] = d_sum[n * 16 + k].astype(jnp.bfloat16).T
        return carry

    lax.fori_loop(0, buckets // 16, turn, 0)
    for r in range(2):
        for b in range(shards * BLOCKS):
            h_turned[:, pl.ds(b * EDGE, EDGE)] = h_sum[r, b].astype(jnp.bfloat16).T
        g_out[r] = jnp.dot(
            h_turned[...],
            a_rows[...].reshape(shards * BLOCKS * EDGE, FEATURE),
            preferred_element_type=jnp.float32,
        )


def local(meta, own_tiles, tiles, a_rows, x_rows, weights):
    buckets = NODES * BLOCKS
    shards = 4
    bf16 = jnp.bfloat16
    return pl.pallas_call(
        local_kernel,
        out_shape=(
            jax.ShapeDtypeStruct((buckets, EDGE, QUARTER), bf16),
            jax.ShapeDtypeStruct((2, QUARTER, FEATURE), jnp.float32),
        ),
        in_specs=[ANY, VMEM, VMEM, VMEM, VMEM, HBM],
        out_specs=(VMEM, VMEM),
        scratch_shapes=[
            pltpu.VMEM((2, QUARTER, FEATURE), bf16),
            pltpu.VMEM((2, shards * BLOCKS, QUARTER, EDGE), bf16),
            pltpu.VMEM((buckets, QUARTER, EDGE), jnp.float32),
            pltpu.VMEM((2, shards * BLOCKS, EDGE, QUARTER), jnp.float32),
            pltpu.VMEM((QUARTER, shards * BLOCKS * EDGE), bf16),
            pltpu.SMEM((shards, 8, TILES), jnp.int32),
            pltpu.SemaphoreType.DMA((2,)),
        ],
        compiler_params=pltpu.CompilerParams(vmem_limit_bytes=24 << 20),
        name="tile_products",
    )(meta, own_tiles, tiles, a_rows, x_rows, weights)


class RingSum:
    def __init__(self, term, send_term, at, peer, got, out, send, recv):
        self.term, self.send_term, self.at, self.peer = term, send_term, at, peer
        self.got, self.out, self.send, self.recv = got, out, send, recv
        self.copies = []

    def place(self, k):
        return lax.rem(self.at + k, SIDE)

    def move(self, view, number, k):
        self.copies.append(
            push(
                view,
                self.got.at[number],
                self.send.at[number],
                self.recv.at[number],
                self.peer(k),
            )
        )

    def begin(self):
        self.move(self.send_term(self.place(2), 0), 0, SIDE - 1)
        self.move(self.send_term(self.place(2), 1), 1, 1)

    def direct(self):
        self.move(self.send_term(self.place(1), 0), 2, 1)
        self.move(self.send_term(self.place(3), 1), 3, SIDE - 1)

    def pass_on(self):
        for number, k, h in ((0, SIDE - 1, 0), (1, 1, 1)):
            arrival(self.got.at[number], self.recv.at[number])
            value = f32(self.term(self.place(k), h)[...]) + f32(self.got[number])
            self.out[h] = value.astype(jnp.bfloat16)
            self.move(self.out.at[h], 4 + h, k)

    def result(self, h):
        for number in (2 + h, 4 + h):
            arrival(self.got.at[number], self.recv.at[number])
        value = f32(self.got[2 + h]) + f32(self.got[4 + h])
        return (value + f32(self.term(self.at, h)[...])).astype(jnp.bfloat16)

    def sent(self):
        for copy in self.copies:
            copy.wait_send()


def f32(value):
    return value.astype(jnp.float32)


def reduce_kernel(
    d_part,
    g_part,
    adj_in,
    self_weight_in,
    g_out,
    d_out,
    got_first,
    out_first,
    got_second,
    summed,
    total,
    got_z,
    got_g,
    adj,
    self_weight,
    local_sem,
    r_send,
    r_recv,
    q_send,
    q_recv,
    z_send,
    z_recv,
    g_send,
    g_recv,
):
    x, y, z, c, rel, node = place()
    quarter = quarter_of(node)
    streams = 4

    def x_peer(k):
        return (lax.rem(x + k, SIDE) * SIDE + y, node)

    def y_peer(k):
        return (x * SIDE + lax.rem(y + k, SIDE), node)

    def fetch(src, dst, sem):
        copy = pltpu.make_async_copy(src, dst, sem)
        copy.start()
        return copy

    get_adj = fetch(adj_in, adj, local_sem.at[0])
    get_weight = fetch(self_weight_in, self_weight, local_sem.at[1])

    def first_ring(stream):
        along_x = stream % 2 == 0

        def view(ref, p, h):
            shards = pl.ds(4 * stream + 2 * h, 2)
            return ref.at[shards, p] if along_x else ref.at[shards, :, p]

        return RingSum(
            lambda p, h: view(d_part, p, h),
            lambda p, h: view(d_part, p, h),
            x if along_x else y,
            x_peer if along_x else y_peer,
            got_first.at[stream],
            out_first.at[stream],
            r_send.at[stream],
            r_recv.at[stream],
        )

    firsts = [first_ring(stream) for stream in range(streams)]

    greet(x, y, rel, node)

    for ring in firsts:
        ring.begin()
    for ring in firsts:
        ring.direct()

    sender = lax.div(z, 2)
    for m in range(4):
        owner = quarter * 4 + m
        rows = g_part.at[:, pl.ds(32 * m, 32), :]

        @pl.when(owner != node)
        def _():
            push(
                rows,
                got_g.at[sender],
                g_send.at[m],
                g_recv.at[sender],
                (rel, owner),
            )

        @pl.when(owner == node)
        def _():
            pltpu.make_async_copy(rows, got_g.at[sender], g_recv.at[sender]).start()

    later = []

    def middle(stream):
        for h in range(2):
            summed[stream, pl.ds(2 * h, 2)] = firsts[stream].result(h)
        at, peer = (y, y_peer) if stream % 2 == 0 else (x, x_peer)
        for k in (2, 1, 3):
            later.append(
                push(
                    summed.at[stream, :, lax.rem(at + k, SIDE)],
                    got_second.at[stream, k - 1],
                    q_send.at[stream, k - 1],
                    q_recv.at[stream, k - 1],
                    peer(k),
                )
            )

    z_copies = []

    def last(stream):
        for k in range(SIDE - 1):
            arrival(got_second.at[stream, k], q_recv.at[stream, k])
        value = f32(summed[stream, :, y if stream % 2 == 0 else x])
        for k in range(SIDE - 1):
            value = value + f32(got_second[stream, k])
        total[pl.ds(4 * stream, 4)] = value.astype(jnp.bfloat16)
        for up in (2 * stream, 2 * stream + 1):
            cores = (1 - c,) if up == 0 else (0, 1)
            for number, core in enumerate(cores):
                z_copies.append(
                    push(
                        total.at[2 * up + core],
                        got_z.at[node],
                        z_send.at[2 * up + number],
                        z_recv.at[2 * up + c],
                        (rel, lax.rem(z + up, 8) * 2 + core),
                    )
                )
        if stream == 0:
            got_z[node] = total[c]

    for ring in firsts:
        ring.pass_on()
    middle(0)
    middle(1)
    middle(2)
    middle(3)
    last(0)
    last(1)
    last(2)
    last(3)

    get_adj.wait()
    get_weight.wait()
    own_term = lax.dot_general(
        adj[...],
        self_weight[...],
        (((1,), (1,)), ((), ())),
        preferred_element_type=jnp.float32,
    )

    for m in range(4):
        arrival(got_g.at[m], g_recv.at[m])
    g_out[...] = (got_g[0] + got_g[1]) + (got_g[2] + got_g[3])

    arrival(got_z.at[z * 2 + 1 - c], z_recv.at[1 - c])
    for up in range(1, 8):
        for core in range(2):
            arrival(
                got_z.at[lax.rem(z + 8 - up, 8) * 2 + core], z_recv.at[2 * up + core]
            )
    for q in range(4):
        value = own_term[:, q * QUARTER : (q + 1) * QUARTER]
        for step in range(4):
            value = value + f32(got_z[(2 * step + q // 2) * 2 + q % 2])
        d_out[:, q * QUARTER : (q + 1) * QUARTER] = value.astype(jnp.bfloat16)

    for ring in firsts:
        ring.sent()
    for copy in later + z_copies:
        copy.wait_send()
    for m in range(4):
        owner = quarter * 4 + m

        @pl.when(owner != node)
        def _():
            pltpu.make_async_remote_copy(
                src_ref=g_part.at[:, pl.ds(32 * m, 32), :],
                dst_ref=got_g.at[sender],
                send_sem=g_send.at[m],
                recv_sem=g_recv.at[sender],
                device_id=(rel, owner),
                device_id_type=MESH,
            ).wait_send()


def reduce(d_part, g_part, adj, self_weight):
    dma = pltpu.SemaphoreType.DMA
    bf16 = jnp.bfloat16
    return pl.pallas_call(
        reduce_kernel,
        out_shape=(
            jax.ShapeDtypeStruct((2, 32, FEATURE), jnp.float32),
            jax.ShapeDtypeStruct((ROWS, FEATURE), bf16),
        ),
        in_specs=[VMEM, VMEM, ANY, ANY],
        out_specs=(VMEM, VMEM),
        scratch_shapes=[
            pltpu.VMEM((4, 6, 2, SIDE, ROWS, QUARTER), bf16),
            pltpu.VMEM((4, 2, 2, SIDE, ROWS, QUARTER), bf16),
            pltpu.VMEM((4, 3, 4, ROWS, QUARTER), bf16),
            pltpu.VMEM((4, 4, SIDE, ROWS, QUARTER), bf16),
            pltpu.VMEM((NODES, ROWS, QUARTER), bf16),
            pltpu.VMEM((NODES, ROWS, QUARTER), bf16),
            pltpu.VMEM((4, 2, 32, FEATURE), jnp.float32),
            pltpu.VMEM((ROWS, FEATURE), bf16),
            pltpu.VMEM((FEATURE, FEATURE), bf16),
            dma((2,)),
            dma((4, 6)),
            dma((4, 6)),
            dma((4, 3)),
            dma((4, 3)),
            dma((16,)),
            dma((16,)),
            dma((4,)),
            dma((4,)),
        ],
        compiler_params=pltpu.CompilerParams(
            collective_id=1, has_side_effects=True, vmem_limit_bytes=24 << 20
        ),
        name="sum_terms",
    )(d_part, g_part, adj, self_weight)


def on_device(
    out_adjoint,
    layer_input,
    rel_weights,
    self_weight,
    tile_values,
    tile_rel,
    tile_target,
    tile_src,
    tile_dest,
):
    code = (
        (tile_dest[:, :, 0] * BLOCKS + tile_src) * 2 + tile_rel
    ) * BLOCKS + tile_target
    meta = jnp.broadcast_to(code, (8, TILES))
    adj = out_adjoint[0]
    stay = functools.partial(
        pltpu.with_memory_space_constraint, memory_space=pltpu.HBM
    )
    tiles, a_rows, x_rows, codes = gather(
        stay(adj),
        stay(layer_input.reshape(SIDE, SIDE, ROWS, FEATURE)),
        stay(tile_values[0]),
        stay(meta),
    )
    d_part, g_part = local(
        codes,
        tile_values[0],
        tiles.reshape(4 * TILES, EDGE, EDGE),
        a_rows.reshape(4 * BLOCKS, EDGE, FEATURE),
        x_rows.reshape(NODES * BLOCKS, EDGE, QUARTER),
        stay(rel_weights),
    )
    rel_weight_grad, d_source = reduce(
        d_part.reshape(NODES, SIDE, SIDE, ROWS, QUARTER), g_part, adj, self_weight
    )
    return rel_weight_grad, d_source[None]


def solution(mesh):
    return jax.shard_map(
        on_device,
        mesh=mesh,
        in_specs=(
            P("node", "rel", None),
            P("node", None, None),
            P("rel", None, None),
            P(),
            P("rel", "node", None, None),
            P("rel", "node"),
            P("rel", "node"),
            P("rel", "node"),
            P("rel", "node", None),
        ),
        out_specs=(P("rel", "node", None), P("node", "rel", None)),
        check_vma=False,
    )
```
